32 devices in a mesh: pre: 2 (over core), dec: 4 (over z), head: 4 (over y, x).
Axes of the slice: x: 2, y: 2, z: 4, core: 2. Of those that a mesh axis runs over, the one named last changes fastest.
Arguments:
- prompt_query: bfloat16 [2, 4096, 32, 128], P('pre', 'dec', 'head'), may hold values from -6 to 6
- prompt_key: bfloat16 [2, 4096, 32, 128], P('pre', 'dec', 'head'), may hold values from -6 to 6
- prompt_value: bfloat16 [2, 4096, 32, 128], P('pre', 'dec', 'head'), may hold values from -6 to 6
- prompt_beta: float32 [2, 32, 4096], P('pre', 'head', 'dec'), may hold values from 0.05 to 0.95
- prompt_gate: float32 [2, 32, 4096], P('pre', 'head', 'dec')
- prompt_lengths: int32 [2, 4], P('pre'), may hold values from 1 to 32, 64 in all within a row
- request_source_prompt: int32 [128], replicated, may hold values from 0 to 7
- live_counts: int32 [8], P(('pre', 'dec')), may hold values from 1 to 16, as said below
- decode_query: bfloat16 [128, 4, 32, 128], P(('pre', 'dec'), None, 'head'), may hold values from -6 to 6
- decode_key: bfloat16 [128, 4, 32, 128], P(('pre', 'dec'), None, 'head'), may hold values from -6 to 6
- decode_value: bfloat16 [128, 4, 32, 128], P(('pre', 'dec'), None, 'head'), may hold values from -6 to 6
- decode_beta: bfloat16 [128, 4, 32], P(('pre', 'dec'), None, 'head'), may hold values from 0.049804688 to 0.94921875
- decode_gate: bfloat16 [128, 4, 32], P(('pre', 'dec'), None, 'head'), may hold values from -0.69921875 to -0.019897461
Outputs:
- prompt_output: bfloat16 [2, 4096, 32, 128], P('pre', 'dec', 'head')
- step_output: bfloat16 [128, 4, 32, 128], P(('pre', 'dec'), None, 'head')
The draws below stay inside these ranges and needn't reach their ends.
Inputs may be any that keep to these rules, and one draw needn't show every extreme that they name: `prompt_lengths`: prompts are packed in order and fill each sequence exactly; in every sequence the longest prompt has 4096 // 128 blocks. `live_counts`: some decoding device has all 16 slots live in every draw; live slots of a device are its first ones.
All inputs are finite; a program needn't handle non-finite values.
Results may differ from the reference program's by a relative error of at most 0.0061.
Values may be sent and summed in bfloat16 or wider, within the bound.
No kernel may reach another device: no remote copies, remote signals or barrier semaphores. Data moves between devices by JAX's collectives and lax.ppermute only.
A program may use at most 128 MiB of HBM per device.

```python
import math
import jax
import jax.numpy as jnp
import numpy as np
from jax import lax

VALUE_HEADS = 32
KEY_SIZE = 128
VALUE_SIZE = 128
SPAN = 64
TOK_DEV = 1024
PROMPTS = 4
SLOTS = 16
DECODE_STEPS = 4
LEN = 4096
SEQS = 2
DECODERS = 8
SLOT_TOTAL = 128
PROMPT_COUNT = 8


def draw_prompt_gate(key, part):
    key = jax.random.fold_in(key, 17)
    keys = jax.random.split(key, 7)
    logarithmic_fading_speed = jax.random.uniform(keys[0], (SEQS, VALUE_HEADS, 1), minval=math.log(0.2 / LEN), maxval=math.log(0.05))
    gaussian_jitter = jax.random.uniform(keys[3], (SEQS, VALUE_HEADS, LEN), minval=0.5, maxval=1.5)
    blocks = LEN // TOK_DEV
    block_log = jax.random.uniform(keys[4], (SEQS, VALUE_HEADS, blocks, 1), minval=math.log(0.5), maxval=math.log(2.0))
    tile_multiplier = jnp.broadcast_to(jnp.exp(block_log), (SEQS, VALUE_HEADS, blocks, TOK_DEV)).reshape(SEQS, VALUE_HEADS, LEN)
    symbol_locations = jax.random.randint(keys[5], (SEQS, 1, 4), 0, LEN)
    update_intensity = jax.random.uniform(keys[6], (SEQS, 1, 4), minval=math.log(0.5), maxval=math.log(0.8))
    element_indices = lax.broadcasted_iota(jnp.int32, (1, 1, LEN, 1), 2)
    span_clusters = jnp.sum(jnp.where(element_indices == symbol_locations[:, :, None, :], update_intensity[:, :, None, :], 0.0), axis=-1)
    return (-jnp.exp(logarithmic_fading_speed) * gaussian_jitter * tile_multiplier + span_clusters).astype(jnp.float32)


def draw_live_counts(key, part):
    key = jax.random.fold_in(key, 29)
    keys = jax.random.split(key, 4)
    first = jax.random.randint(keys[0], (DECODERS,), 1, SLOTS + 1)
    second = jax.random.randint(keys[1], (DECODERS,), 1, SLOTS + 1)
    third = jax.random.randint(keys[2], (DECODERS,), 1, SLOTS + 1)
    lowest = jnp.minimum(jnp.minimum(first, second), third)
    fullest = jax.random.randint(keys[3], (), 0, DECODERS)
    return jnp.where(jnp.arange(DECODERS, dtype=jnp.int32) == fullest, SLOTS, lowest).astype(jnp.int32)


def set_ends(values, key, smallest, high):
    dims = values.shape
    place = [jax.random.randint(jax.random.fold_in(key, axis), (), 0, dims[axis]) for axis in range(len(dims))]
    values = values.at[tuple(place)].set(smallest)
    longest = dims.index(max(dims))
    place[longest] = (place[longest] + 1) % dims[longest]
    return values.at[tuple(place)].set(high)


def levels(own_key, dims, cuts, low, high):
    gain, own = 1.0, jax.random.fold_in(own_key, 6)
    for axis_at, parts in cuts:
        heights = jnp.exp(jax.random.uniform(jax.random.fold_in(own, axis_at), (parts,), jnp.float32, low / len(cuts), high / len(cuts)))
        gain = gain * jnp.repeat(heights, dims[axis_at] // parts).reshape([-1 if axis == axis_at else 1 for axis in range(len(dims))])
    return gain


def length_profile(count, total, most, skew):
    portions = [(1 << 20) // math.isqrt(standing ** skew) + 1 for standing in range(2, count + 1)]
    spare, given = total - most - (count - 1), [1] * (count - 1)
    while spare > 0:
        free = [i for i in range(count - 1) if given[i] < most]
        mass, left = sum([portions[i] for i in free]), spare
        for i in free:
            addition = min(most - given[i], max(1, left * portions[i] // mass), spare)
            given[i] = given[i] + addition
            spare = spare - addition
    return np.array([most] + given)


def uneven(own_key, amount, total, most, lean):
    if amount == 2:
        one = jax.random.randint(own_key, (), max(1, total - most), min(most, total - 1) + 1)
        return jnp.stack([one, total - one])
    sizes = jnp.asarray(length_profile(amount, total, most, lean), jnp.int32)
    pairs = (amount - 1) // 2
    source_of, receiver = sizes[1:1 + 2 * pairs:2], sizes[2:2 + 2 * pairs:2]
    margin = jnp.minimum(source_of - 1, most - receiver)
    passed = jax.random.randint(jax.random.fold_in(own_key, 1), (pairs,), 0, 1 << 20) % (margin + 1)
    sizes = sizes.at[1:1 + 2 * pairs:2].set(source_of - passed).at[2:2 + 2 * pairs:2].set(receiver + passed)
    return sizes[jax.random.permutation(jax.random.fold_in(own_key, 2), amount)]


def normal_values(rng, extent, width, reach, cuts=(), held_as=jnp.bfloat16):
    result = jax.random.normal(rng, extent, jnp.float32) * width
    if len(cuts) > 0:
        result = levels(rng, extent, cuts, -0.22, 0.18) * result
    return jnp.clip(result, min=-reach, max=reach).astype(held_as)


def setup_inputs(seed: int = 0) -> dict:
    key_of = jax.random.split(jax.random.key(seed), 14)
    prompt_query = normal_values(key_of[0], (SEQS, LEN, VALUE_HEADS, KEY_SIZE), 1.0, 6.0, ((0, 2), (1, 4), (2, 4)))
    prompt_key = normal_values(key_of[1], (SEQS, LEN, VALUE_HEADS, KEY_SIZE), 1.0, 6.0, ((0, 2), (1, 4), (2, 4)))
    prompt_value = normal_values(key_of[2], (SEQS, LEN, VALUE_HEADS, VALUE_SIZE), 1.0, 6.0, ((0, 2), (1, 4), (2, 4)))
    prompt_beta = jnp.clip(0.05 + 0.9 * jax.random.uniform(key_of[3], (SEQS, VALUE_HEADS, LEN), jnp.float32) ** levels(key_of[3], (SEQS, VALUE_HEADS, LEN), ((0, 2), (1, 4), (2, 4)), -0.2, 0.2), 0.05, 0.95)
    prompt_gate = draw_prompt_gate(jax.random.fold_in(key_of[13], 71), 0)
    prompt_lengths = jax.vmap(lambda own: uneven(own, PROMPTS, LEN // SPAN, LEN // (2 * SPAN), 2))(jax.random.split(key_of[5], SEQS)).reshape((SEQS, PROMPTS)).astype(jnp.int32)
    request_source_prompt = set_ends(jax.random.randint(key_of[6], (SLOT_TOTAL,), 0, PROMPT_COUNT), jax.random.fold_in(key_of[6], 1), 0, PROMPT_COUNT - 1).astype(jnp.int32)
    live_counts = draw_live_counts(jax.random.fold_in(key_of[13], 71), 0)
    decode_query = normal_values(key_of[8], (SLOT_TOTAL, DECODE_STEPS, VALUE_HEADS, KEY_SIZE), 1.0, 6.0, ((0, 8), (2, 4)))
    decode_key = normal_values(key_of[9], (SLOT_TOTAL, DECODE_STEPS, VALUE_HEADS, KEY_SIZE), 1.0, 6.0, ((0, 8), (2, 4)))
    decode_value = normal_values(key_of[10], (SLOT_TOTAL, DECODE_STEPS, VALUE_HEADS, VALUE_SIZE), 1.0, 6.0, ((0, 8), (2, 4)))
    decode_beta = jnp.clip(0.049804688 + 0.89941406 * jax.random.uniform(key_of[11], (SLOT_TOTAL, DECODE_STEPS, VALUE_HEADS), jnp.float32) ** levels(key_of[11], (SLOT_TOTAL, DECODE_STEPS, VALUE_HEADS), ((0, 8), (2, 4)), -0.2, 0.2), 0.049804688, 0.94921875).astype(jnp.bfloat16)
    decode_gate = jnp.clip(-0.69921875 + 0.6793213 * jax.random.uniform(key_of[12], (SLOT_TOTAL, DECODE_STEPS, VALUE_HEADS), jnp.float32) ** levels(key_of[12], (SLOT_TOTAL, DECODE_STEPS, VALUE_HEADS), ((0, 8), (2, 4)), -0.2, 0.2), -0.69921875, -0.019897461).astype(jnp.bfloat16)
    return dict(prompt_query=prompt_query, prompt_key=prompt_key, prompt_value=prompt_value, prompt_beta=prompt_beta, prompt_gate=prompt_gate, prompt_lengths=prompt_lengths, request_source_prompt=request_source_prompt, live_counts=live_counts, decode_query=decode_query, decode_key=decode_key, decode_value=decode_value, decode_beta=decode_beta, decode_gate=decode_gate)


exact_dots = lax.Precision.HIGHEST

def unit_rows(source):
    widened = source.astype(jnp.float32)
    return widened * lax.rsqrt(lax.optimization_barrier(jnp.sum(widened * widened, axis=-1, keepdims=True)) + 1e-06)

def inverse_norms(source):
    widened = source.astype(jnp.float32)
    return jnp.transpose(lax.rsqrt(lax.optimization_barrier(jnp.sum(widened * widened, axis=-1)) + 1e-06), (0, 2, 1))

def span_terms(query_rows, key_rows, values, beta_rows, log_gate):
    block_size = key_rows.shape[1]
    q_unit = unit_rows(query_rows)
    k_unit = unit_rows(key_rows)
    k_scale = inverse_norms(key_rows)
    q_scale = inverse_norms(query_rows)
    cum_gate = jnp.transpose(jnp.cumsum(log_gate, axis=2), (1, 0, 2))
    betas = jnp.transpose(beta_rows, (1, 0, 2))
    row_ids = lax.broadcasted_iota(jnp.int32, (block_size, block_size), 0)
    col_ids = lax.broadcasted_iota(jnp.int32, (block_size, block_size), 1)
    on_lower = row_ids >= col_ids
    log_gap = jnp.where(on_lower, cum_gate[:, :, :, None] - cum_gate[:, :, None, :], 0.0)
    decays = jnp.where(on_lower, jnp.exp(log_gap), 0.0)
    raw_gram = jnp.einsum('nihd,njhd->nhij', key_rows, key_rows, preferred_element_type=jnp.float32)
    key_gram = raw_gram * k_scale[:, :, :, None] * k_scale[:, :, None, :]
    strict_part = jnp.where(row_ids > col_ids, betas[:, :, :, None] * decays * key_gram, 0.0)
    identity = jnp.eye(block_size, dtype=jnp.float32)
    powered = strict_part
    inverse = identity - strict_part
    for rounds in range(int(math.log2(block_size)) - 1):
        powered = jnp.matmul(powered, powered, precision=exact_dots)
        inverse = jnp.matmul(inverse, identity + powered, precision=exact_dots)
    inverse_half = inverse.astype(jnp.bfloat16)
    growth = jnp.exp(cum_gate)
    weighted = (k_unit * jnp.swapaxes(betas * growth, 1, 2)[..., None]).astype(jnp.bfloat16)
    w_rows = jnp.einsum('nhij,njhd->nhid', inverse_half, weighted, preferred_element_type=jnp.float32)
    scaled_values = (values.astype(jnp.float32) * jnp.swapaxes(betas, 1, 2)[..., None]).astype(jnp.bfloat16)
    u_rows = jnp.einsum('nhij,njhd->nhid', inverse_half, scaled_values, preferred_element_type=jnp.float32)
    q_grown = q_unit * jnp.swapaxes(growth, 1, 2)[..., None]
    raw_scores = jnp.einsum('nihd,njhd->nhij', query_rows, key_rows, preferred_element_type=jnp.float32)
    scores = raw_scores * q_scale[:, :, :, None] * k_scale[:, :, None, :] * decays
    k_tail = k_unit * jnp.swapaxes(jnp.exp(cum_gate[:, :, -1:] - cum_gate), 1, 2)[..., None]
    span_decay = growth[:, :, -1]
    return (q_grown, scores, w_rows, u_rows, k_tail, span_decay)

def fresh_of(piece, entry):
    return piece[3] - jnp.einsum('hid,hde->hie', piece[2], entry, precision=exact_dots)

def emit_of(piece, entry, fresh_part):
    first = jnp.einsum('ihd,hde->ihe', piece[0], entry, precision=exact_dots)
    return first + jnp.einsum('hij,hje->ihe', piece[1], fresh_part, precision=exact_dots)

def leave_of(piece, entry, fresh_part):
    carried = piece[5][:, None, None] * entry
    return carried + jnp.einsum('ihd,hie->hde', piece[4], fresh_part, precision=exact_dots)

def reference(prompt_query, prompt_key, prompt_value, prompt_beta, prompt_gate, prompt_lengths, request_source_prompt, live_counts, decode_query, decode_key, decode_value, decode_beta, decode_gate):

    def one_sequence(inputs):
        query_rows, key_rows, value_rows, beta_rows, gate_rows, lengths = inputs
        span_count = LEN // SPAN
        span_parts = span_terms(query_rows.reshape(span_count, SPAN, VALUE_HEADS, KEY_SIZE), key_rows.reshape(span_count, SPAN, VALUE_HEADS, KEY_SIZE), value_rows.reshape(span_count, SPAN, VALUE_HEADS, VALUE_SIZE), beta_rows.reshape(VALUE_HEADS, span_count, SPAN), gate_rows.reshape(VALUE_HEADS, span_count, SPAN))
        end_spans = jnp.cumsum(lengths).astype(jnp.int32) - 1
        starts = end_spans + 1 - lengths
        span_ids = jnp.arange(span_count, dtype=jnp.int32)
        keep_flags = 1.0 - jnp.any(span_ids[:, None] == starts[None, :], axis=1).astype(jnp.float32)

        def walk(carry, slices):
            state, end_table = carry
            piece, keep, span_id = slices
            entry = keep * state
            fresh_part = fresh_of(piece, entry)
            output = emit_of(piece, entry, fresh_part)
            leaving = leave_of(piece, entry, fresh_part)
            hit = (end_spans == span_id)[:, None, None, None]
            end_table = jnp.where(hit, leaving[None], end_table)
            return ((leaving, end_table), output)
        start_carry = (jnp.zeros((VALUE_HEADS, KEY_SIZE, VALUE_SIZE), jnp.float32), jnp.zeros((PROMPTS, VALUE_HEADS, KEY_SIZE, VALUE_SIZE), jnp.float32))
        (last_state, end_table), outputs = lax.scan(walk, start_carry, (span_parts, keep_flags, span_ids))
        return (outputs.reshape(LEN, VALUE_HEADS, VALUE_SIZE).astype(jnp.bfloat16), end_table.astype(jnp.bfloat16))
    prompt_result, tables = lax.map(one_sequence, (prompt_query, prompt_key, prompt_value, prompt_beta, prompt_gate, prompt_lengths))
    tables_flat = tables.reshape(PROMPT_COUNT, VALUE_HEADS, KEY_SIZE, VALUE_SIZE)

    def decode_block(inputs):
        chosen, query_rows, key_rows, value_rows, beta_rows, gate_rows, limit = inputs
        state = jnp.take(tables_flat, chosen, axis=0).astype(jnp.float32)
        q_unit = unit_rows(query_rows)
        k_unit = unit_rows(key_rows)
        outputs = []
        for moment in range(DECODE_STEPS):
            state = jnp.exp(gate_rows[:, moment].astype(jnp.float32))[:, :, None, None] * state
            predicted = jnp.einsum('bhd,bhde->bhe', k_unit[:, moment], state, precision=exact_dots)
            update = beta_rows[:, moment].astype(jnp.float32)[..., None] * (value_rows[:, moment].astype(jnp.float32) - predicted)
            state = state + k_unit[:, moment][..., None] * update[:, :, None, :]
            outputs.append(jnp.einsum('bhd,bhde->bhe', q_unit[:, moment], state, precision=exact_dots))
        stacked = jnp.stack(outputs, axis=1)
        live_slots = jnp.arange(SLOTS, dtype=jnp.int32) < limit
        return jnp.where(live_slots[:, None, None, None], stacked, 0.0).astype(jnp.bfloat16)
    decode_result = lax.map(decode_block, (request_source_prompt.reshape(DECODERS, SLOTS), decode_query.reshape(DECODERS, SLOTS, DECODE_STEPS, VALUE_HEADS, KEY_SIZE), decode_key.reshape(DECODERS, SLOTS, DECODE_STEPS, VALUE_HEADS, KEY_SIZE), decode_value.reshape(DECODERS, SLOTS, DECODE_STEPS, VALUE_HEADS, VALUE_SIZE), decode_beta.reshape(DECODERS, SLOTS, DECODE_STEPS, VALUE_HEADS), decode_gate.reshape(DECODERS, SLOTS, DECODE_STEPS, VALUE_HEADS), live_counts))
    return (prompt_result, decode_result.reshape(SLOT_TOTAL, DECODE_STEPS, VALUE_HEADS, VALUE_SIZE))
```

```python
import functools

import jax
import jax.numpy as jnp
from jax import lax
from jax.experimental import pallas as pl
from jax.experimental.pallas import tpu as pltpu
from jax.sharding import PartitionSpec as P

SPAN = 64
PROMPTS = 4
F32 = jnp.float32
BF16 = jnp.bfloat16
MIB = 1024 * 1024
VMEM_BYTES = 60 * MIB
BASE = 32
SUBS = 2


def dot(left, right):
    return jnp.dot(left, right, preferred_element_type=F32)


def dot_last(left, right):
    return lax.dot_general(left, right, (((1,), (1,)), ((), ())), preferred_element_type=F32)


def scale_of(rows):
    return lax.rsqrt(jnp.sum(rows * rows, axis=-1, keepdims=True) + 1e-06)


def unit(rows):
    return rows * scale_of(rows)


def iota2(shape, dim):
    return lax.broadcasted_iota(jnp.int32, shape, dim)


def any_equal(marks, value):
    found = marks[0] == value
    for mark in marks[1:]:
        found = jnp.logical_or(found, mark == value)
    return found


def prompt_ends(lengths):
    ends = [lengths[0, 0] - 1]
    for j in range(1, PROMPTS):
        ends.append(ends[-1] + lengths[0, j])
    return ends


def first_end_in(ends, first, count):
    found = jnp.int32(count)
    for end in reversed(ends):
        inside = jnp.logical_and(end >= first, end < first + count)
        found = jnp.where(inside, end - first, found)
    return found


def tiled(part, size):
    return jnp.concatenate([part] * (size // part.shape[0]), axis=0)


def inverse_of(lower, masks, group):
    size = lower[0].shape[0]
    heads = range(group)
    zero = jnp.zeros((size, size), BF16)

    def packed(h, width):
        parts = [
            jnp.where(masks["lanes", width, b], lower[h][b * width : (b + 1) * width], 0.0)
            for b in range(size // width)
        ]
        return functools.reduce(lambda x, y: x + y, parts)

    def spread(part, mask):
        return jnp.where(mask, tiled(part, size), zero)

    small = [packed(h, BASE) for h in heads]
    inverse = [masks["eye"] - small[h] for h in heads]
    part = [small[h].astype(BF16) for h in heads]
    full = [spread(part[h], masks["same", BASE]) for h in heads]
    part = [dot(part[h], full[h]).astype(BF16) for h in heads]
    power = 2
    while power < BASE:
        full = [spread(part[h], masks["same", BASE]) for h in heads]
        if 2 * power < BASE:
            both = [
                dot(jnp.concatenate([part[h], inverse[h].astype(BF16)], axis=0), full[h])
                for h in heads
            ]
            part = [both[h][:BASE].astype(BF16) for h in heads]
            inverse = [inverse[h] + both[h][BASE:] for h in heads]
        else:
            inverse = [inverse[h] + dot(inverse[h].astype(BF16), full[h]) for h in heads]
        power *= 2
    inverse = [inverse[h].astype(BF16) for h in heads]
    full = [spread(inverse[h], masks["same", BASE]) for h in heads]
    width = BASE
    while width < size:
        below = []
        for h in heads:
            parts = [
                jnp.where(
                    masks["lanes", width, 2 * b],
                    lower[h][(2 * b + 1) * width : (2 * b + 2) * width],
                    0.0,
                )
                for b in range(size // (2 * width))
            ]
            below.append(functools.reduce(lambda x, y: x + y, parts).astype(BF16))
        turned = [dot(below[h], full[h]).astype(BF16) for h in heads]
        wide = [spread(turned[h], masks["off", width]) for h in heads]
        corner = [-dot(inverse[h], wide[h]) for h in heads]
        even = masks["even", width]
        corner = [corner[h].astype(BF16) for h in heads]
        inverse = [
            jnp.concatenate(
                [
                    jnp.where(even, inverse[h], jnp.zeros_like(inverse[h])),
                    jnp.where(even, corner[h], inverse[h]),
                ],
                axis=0,
            )
            for h in heads
        ]
        width *= 2
        if width < size:
            full = [spread(inverse[h], masks["same", width]) for h in heads]
    return inverse


def masks_of(size):
    row = iota2((size, size), 0)
    col = iota2((size, size), 1)
    masks = {"eye": (iota2((BASE, size), 0) == iota2((BASE, size), 1) % BASE).astype(F32)}
    width = BASE
    while width < size:
        masks["same", width] = (row // width) == (col // width)
        masks["off", width] = jnp.logical_and(
            (row // (2 * width)) == (col // (2 * width)), (row // width) != (col // width)
        )
        lanes = iota2((width, size), 1) // width
        for b in range(size // width):
            masks["lanes", width, b] = lanes == b
        masks["even", width] = lanes % 2 == 0
        width *= 2
    return masks


def chunk_kernel(
    spans,
    lengths,
    q_ref,
    k_ref,
    v_ref,
    beta_ref,
    gate_ref,
    local_ref,
    probe_ref,
    state_ref,
    sent_ref,
    map_ref,
    table_ref,
    qf,
    kf,
    vf,
    walk,
    fresh,
    turned_keys,
):
    turn = pl.program_id(0)
    block_rows, heads, width = k_ref.shape
    rows = 2 * SPAN
    subs = block_rows // rows
    half = rows // 2
    places = 2 * subs

    @pl.when(turn == 0)
    def _():
        eye = (iota2((width, width), 0) == iota2((width, width), 1)).astype(F32)
        for h in range(heads):
            walk[0, h, :, :width] = jnp.zeros((width, width), F32)
            walk[0, h, :, width:] = eye
        table_ref[...] = jnp.zeros_like(table_ref)

    base = lax.axis_index("dec") * spans
    ends = [end - base for end in prompt_ends(lengths)]
    starts = [-base] + [end + 1 for end in ends[:-1]]
    map_block = jnp.minimum(first_end_in(ends, 0, spans), spans - 1)
    first_place = lax.rem(turn, 2) * subs
    first_block = 2 * subs * turn
    keeps = [
        1.0 - any_equal(starts, first_block + i).astype(F32)
        for i in range(2 * subs)
    ]

    qf[...] = q_ref[...].astype(F32).reshape(block_rows * heads, width)
    kf[...] = k_ref[...].astype(F32).reshape(block_rows * heads, width)
    vf[...] = v_ref[...].astype(F32).reshape(block_rows * heads, width)

    row = iota2((rows, rows), 0)
    col = iota2((rows, rows), 1)
    strict = row > col
    diagonal = row == col
    masks = masks_of(rows)
    lowers, row_opens, lane_opens, totals, total_cols, beta_cols = [], [], [], [], [], []
    for s in range(subs):
        keep1 = keeps[2 * s + 1]
        open_pair = jnp.logical_or(
            (row >= half) == (col >= half), jnp.full((rows, rows), keep1) > 0.5
        )
        lowers.append(jnp.logical_and(row >= col, open_pair))
        row_opens.append(jnp.where(iota2((rows, 1), 0) >= half, keep1, 1.0))
        lane_opens.append(jnp.where(iota2((1, rows), 1) < half, keep1, 1.0))
        total = lax.dot_general(
            gate_ref[:, s * rows : (s + 1) * rows],
            (row <= col).astype(F32),
            (((1,), (0,)), ((), ())),
            precision=lax.Precision.HIGHEST,
            preferred_element_type=F32,
        )
        totals.append(total)
        total_cols.append(jnp.transpose(total))
        beta_cols.append(jnp.transpose(beta_ref[:, s * rows : (s + 1) * rows]))

    units = [(s, h) for s in range(subs) for h in range(heads)]
    idx = range(len(units))

    def rows_of(ref, s, h):
        return ref[pl.ds(s * rows * heads + h, rows, stride=heads), :]

    keys = [rows_of(kf, s, h) for s, h in units]
    queries = [rows_of(qf, s, h) for s, h in units]
    keys_half = [x.astype(BF16) for x in keys]
    queries_half = [x.astype(BF16) for x in queries]
    grams = [
        dot_last(jnp.concatenate([keys_half[i], queries_half[i]], axis=0), keys_half[i])
        for i in idx
    ]
    key_col = [scale_of(keys[i]) for i in idx]
    query_col = [scale_of(queries[i]) for i in idx]
    key_row = [
        lax.rsqrt(
            jnp.sum(jnp.where(diagonal, grams[i][:rows], 0.0), axis=0, keepdims=True) + 1e-06
        )
        for i in idx
    ]
    sums_col = [total_cols[s][:, h : h + 1] for s, h in units]
    sums_row = [totals[s][h : h + 1, :] for s, h in units]
    betas = [beta_cols[s][:, h : h + 1] for s, h in units]
    decays = [
        jnp.exp(jnp.where(lowers[units[i][0]], sums_col[i] - sums_row[i], -1e30)) * key_row[i]
        for i in idx
    ]
    strict_part = [
        jnp.where(strict, (betas[i] * key_col[i]) * (decays[i] * grams[i][:rows]), 0.0)
        for i in idx
    ]
    scores = [(query_col[i] * (decays[i] * grams[i][rows:])).astype(BF16) for i in idx]
    growth = [jnp.exp(sums_col[i]) * row_opens[units[i][0]] for i in idx]
    inverse = inverse_of(strict_part, masks, len(units))
    right = [
        jnp.concatenate(
            [
                (keys[i] * (betas[i] * growth[i] * key_col[i])).astype(BF16),
                (rows_of(vf, *units[i]) * betas[i]).astype(BF16),
            ],
            axis=1,
        )
        for i in idx
    ]
    wu = [dot(inverse[i], right[i]) for i in idx]
    turned = [jnp.transpose(keys[i]) * key_row[i] for i in idx]
    tails = [
        (
            turned[i]
            * (jnp.exp(sums_row[i][:, rows - 1 :] - sums_row[i]) * lane_opens[units[i][0]])
        ).astype(BF16)
        for i in idx
    ]
    grown = [(queries[i] * (growth[i] * query_col[i])).astype(BF16) for i in idx]
    entry = [walk[first_place, h] for h in range(heads)]
    for s in range(subs):
        mine = [s * heads + h for h in range(heads)]
        entry = [x * keeps[2 * s] for x in entry]
        entry_half = [x.astype(BF16) for x in entry]
        moved = [dot(wu[i][:, :width].astype(BF16), entry_half[i % heads]) for i in mine]
        new = [
            jnp.concatenate(
                [
                    wu[i][:, width:] - moved[i % heads][:, :width],
                    -moved[i % heads][:, width:],
                ],
                axis=1,
            ).astype(BF16)
            for i in mine
        ]
        leaving = [
            entry[i % heads] * (jnp.exp(sums_row[i][:, rows - 1 :]) * keeps[2 * s + 1])
            + dot(tails[i], new[i % heads])
            for i in mine
        ]
        outs = [
            dot(
                jnp.concatenate([grown[i], scores[i]], axis=1),
                jnp.concatenate([entry_half[i % heads], new[i % heads]], axis=0),
            )
            for i in mine
        ]
        place = lax.rem(first_place + s + 1, places)
        for h in range(heads):
            walk[place, h] = leaving[h]
            fresh[s, h] = new[h]
            turned_keys[s, h] = turned[mine[h]]
            local_ref[h, s * rows : (s + 1) * rows] = outs[h][:, :width]
            probe_ref[h, s * rows : (s + 1) * rows] = outs[h][:, width:].astype(BF16)
        entry = leaving

    for s in range(subs):
        block0 = first_block + 2 * s
        now = lax.rem(first_place + s, places)
        later = lax.rem(first_place + s + 1, places)

        @pl.when(jnp.logical_or(any_equal(ends, block0), map_block == block0))
        def _(s=s, block0=block0, now=now):
            for h in range(heads):
                row_sums = totals[s][h : h + 1, :]
                at_half = row_sums[:, half - 1 : half]
                lanes = iota2((1, rows), 1)
                weight = jnp.exp(jnp.where(lanes < half, at_half - row_sums, -1e30))
                state = walk[now, h] * (keeps[2 * s] * jnp.exp(at_half)) + dot(
                    (turned_keys[s, h] * weight).astype(BF16), fresh[s, h]
                )
                for j in range(PROMPTS):

                    @pl.when(ends[j] == block0)
                    def _(j=j, h=h, state=state):
                        table_ref[j, h] = state[:, :width].astype(BF16)

                @pl.when(map_block == block0)
                def _(h=h, state=state):
                    map_ref[h] = state[:, width:].astype(BF16)

        for j in range(PROMPTS):

            @pl.when(ends[j] == block0 + 1)
            def _(j=j, later=later):
                table_ref[j] = walk[later, :, :, :width].astype(BF16)

        @pl.when(map_block == block0 + 1)
        def _(later=later):
            map_ref[...] = walk[later, :, :, width:].astype(BF16)

    @pl.when(turn == pl.num_programs(0) - 1)
    def _():
        last = walk[lax.rem(first_place + subs, places), :, :, :width]
        state_ref[...] = last
        sent_ref[...] = last.astype(BF16)


def prefill(lengths, query, key, value, beta, gate):
    tokens, heads, width = key.shape
    rows = 2 * SPAN * SUBS
    token_spec = pl.BlockSpec((rows, heads, width), lambda c, s: (c, 0, 0))
    gate_spec = pl.BlockSpec((heads, rows), lambda c, s: (0, c))
    out_spec = pl.BlockSpec((heads, rows, width), lambda c, s: (0, c, 0))
    whole = pl.BlockSpec((heads, width, width), lambda c, s: (0, 0, 0))
    table_spec = pl.BlockSpec((PROMPTS, heads, width, width), lambda c, s: (0, 0, 0, 0))
    return pl.pallas_call(
        functools.partial(chunk_kernel, tokens // SPAN),
        grid_spec=pltpu.PrefetchScalarGridSpec(
            num_scalar_prefetch=1,
            grid=(tokens // rows,),
            in_specs=[token_spec, token_spec, token_spec, gate_spec, gate_spec],
            out_specs=[out_spec, out_spec, whole, whole, whole, table_spec],
            scratch_shapes=[
                pltpu.VMEM((rows * heads, width), F32),
                pltpu.VMEM((rows * heads, width), F32),
                pltpu.VMEM((rows * heads, width), F32),
                pltpu.VMEM((2 * SUBS, heads, width, 2 * width), F32),
                pltpu.VMEM((SUBS, heads, 2 * SPAN, 2 * width), BF16),
                pltpu.VMEM((SUBS, heads, width, 2 * SPAN), F32),
            ],
        ),
        out_shape=[
            jax.ShapeDtypeStruct((heads, tokens, width), F32),
            jax.ShapeDtypeStruct((heads, tokens, width), BF16),
            jax.ShapeDtypeStruct((heads, width, width), F32),
            jax.ShapeDtypeStruct((heads, width, width), BF16),
            jax.ShapeDtypeStruct((heads, width, width), BF16),
            jax.ShapeDtypeStruct((PROMPTS, heads, width, width), BF16),
        ],
        compiler_params=pltpu.CompilerParams(vmem_limit_bytes=VMEM_BYTES),
        cost_estimate=pl.CostEstimate(flops=6 * 10**9, bytes_accessed=16 * MIB, transcendentals=0),
        name="chunks",
    )(lengths, query, key, value, beta, gate)


def request_kernel(q_ref, k_ref, v_ref, scale_ref, probe_ref, local_ref, rows_ref):
    slots, steps, heads, width = q_ref.shape
    keys = [unit(k_ref[:, t].astype(F32)) for t in range(steps)]
    queries = [unit(q_ref[:, t].astype(F32)) for t in range(steps)]
    gates = []
    for t in range(steps):
        gate = scale_ref[1, t]
        gates.append(gate if t == 0 else gates[-1] + gate)
    weights, updates = [], []
    for t in range(steps):
        beta = scale_ref[0, t]
        reach = jnp.exp(gates[t]) * keys[t]
        value = v_ref[:, t].astype(F32)
        for s in range(t):
            factor = jnp.exp(gates[t] - gates[s]) * jnp.sum(keys[s] * keys[t], axis=-1, keepdims=True)
            reach = reach - factor * weights[s]
            value = value - factor * updates[s]
        weights.append(beta * reach)
        updates.append(beta * value)
        probe = jnp.exp(gates[t]) * queries[t]
        emitted = jnp.zeros_like(value)
        for s in range(t + 1):
            factor = jnp.sum(keys[s] * queries[t], axis=-1, keepdims=True)
            factor = factor if s == t else factor * jnp.exp(gates[t] - gates[s])
            probe = probe - factor * weights[s]
            emitted = emitted + factor * updates[s]
        rows_ref[pl.ds(t * slots * heads, slots * heads), :] = probe.reshape(slots * heads, width)
        local_ref[t] = emitted
    for h in range(heads):
        probe_ref[h] = rows_ref[pl.ds(h, steps * slots, stride=heads), :].astype(BF16)


def requests(query, key, value, beta, gate):
    slots, steps, heads, width = query.shape
    scales = jnp.transpose(jnp.stack([beta, gate]).astype(F32), (0, 2, 1, 3))[..., None]
    return pl.pallas_call(
        request_kernel,
        out_shape=[
            jax.ShapeDtypeStruct((heads, steps * slots, width), BF16),
            jax.ShapeDtypeStruct((steps, slots, heads, width), F32),
        ],
        scratch_shapes=[pltpu.VMEM((steps * slots * heads, width), F32)],
        compiler_params=pltpu.CompilerParams(vmem_limit_bytes=VMEM_BYTES),
        name="requests",
    )(query, key, value, scales)


def reversed_bits(value, count):
    bits, turned = count.bit_length() - 1, 0
    for i in range(bits):
        turned |= ((value >> i) & 1) << (bits - 1 - i)
    return turned


def answer_kernel(
    spans,
    lengths,
    state_ref,
    map_ref,
    arrived_ref,
    next_map_ref,
    table_ref,
    probe_ref,
    source_ref,
    sent_ref,
    keep_ref,
    send_ref,
    source_rows,
    left,
    total,
):
    _, peers, _, rows, width = probe_ref.shape
    me, mine = lax.axis_index("dec"), lax.axis_index("pre")
    ends = prompt_ends(lengths)
    base = me * spans
    places = [
        (p, x, lax.rem(mine + p, 2), jnp.bitwise_xor(me, reversed_bits(x, peers)))
        for p in range(2)
        for x in range(peers)
    ]

    @pl.when(pl.program_id(0) == 0)
    def _():
        for i, (_, _, pre, peer) in enumerate(places):
            source_rows[i * rows : (i + 1) * rows, :] = jnp.broadcast_to(
                source_ref[pre, peer], (rows, width)
            )

    for i, (_, _, pre, peer) in enumerate(places):
        left[i * rows : (i + 1) * rows, :] = probe_ref[pre, peer, 0]
    closed = first_end_in(ends, base, spans) < spans
    through = jnp.where(closed, 0.0, 1.0)
    leaving = state_ref[0] + through * dot(map_ref[0], arrived_ref[0])
    leaving_half = leaving.astype(BF16)
    sent_ref[0] = leaving_half
    carried = dot(next_map_ref[0], leaving_half).astype(BF16)
    next_end = base + spans + first_end_in(ends, base + spans, spans)
    next_prompt = jnp.int32(-1)
    for j in range(PROMPTS):
        next_prompt = jnp.where(ends[j] == next_end, mine * PROMPTS + j, next_prompt)
    total[...] = jnp.where(source_rows[...] == next_prompt, dot(left[...], carried), 0.0)
    for j in range(PROMPTS):

        @pl.when(jnp.logical_and(ends[j] >= base, ends[j] < base + spans))
        def _(j=j):
            total[...] = jnp.where(
                source_rows[...] == mine * PROMPTS + j, dot(left[...], table_ref[j, 0]), total[...]
            )

    size = peers * rows
    keep_ref[:, 0] = total[:size].astype(BF16).reshape(peers, rows, width)
    send_ref[:, 0] = total[size:].astype(BF16).reshape(peers, rows, width)


def answers(lengths, spans, state, own_map, arrived, next_map, table, probes, sources):
    _, peers, heads, rows, width = probes.shape
    per_head = pl.BlockSpec((1, width, width), lambda h, s: (h, 0, 0))
    table_spec = pl.BlockSpec((PROMPTS, 1, width, width), lambda h, s: (0, h, 0, 0))
    probe_spec = pl.BlockSpec((2, peers, 1, rows, width), lambda h, s: (0, 0, h, 0, 0))
    out_spec = pl.BlockSpec((peers, 1, rows, width), lambda h, s: (0, h, 0, 0))
    source_spec = pl.BlockSpec((2, peers, rows, 1), lambda h, s: (0, 0, 0, 0))
    out = jax.ShapeDtypeStruct((peers, heads, rows, width), BF16)
    return pl.pallas_call(
        functools.partial(answer_kernel, spans),
        grid_spec=pltpu.PrefetchScalarGridSpec(
            num_scalar_prefetch=1,
            grid=(heads,),
            in_specs=[per_head] * 4 + [table_spec, probe_spec, source_spec],
            out_specs=[per_head, out_spec, out_spec],
            scratch_shapes=[
                pltpu.VMEM((2 * peers * rows, width), jnp.int32),
                pltpu.VMEM((2 * peers * rows, width), BF16),
                pltpu.VMEM((2 * peers * rows, width), F32),
            ],
        ),
        out_shape=[jax.ShapeDtypeStruct((heads, width, width), BF16), out, out],
        compiler_params=pltpu.CompilerParams(vmem_limit_bytes=VMEM_BYTES),
        name="answers",
    )(lengths, state, own_map, arrived, next_map, table, probes, sources)


def emit_kernel(local_ref, probe_ref, entry_ref, out_ref, rows_ref):
    heads, rows, width = local_ref.shape
    for h in range(heads):
        rows_ref[pl.ds(h, rows, stride=heads), :] = local_ref[h] + dot(probe_ref[h], entry_ref[h])
    out_ref[...] = rows_ref[...].reshape(rows, heads, width).astype(BF16)


def emit(local, probe, entry):
    heads, tokens, width = local.shape
    rows = 2 * SPAN
    spec = pl.BlockSpec((heads, rows, width), lambda c: (0, c, 0))
    return pl.pallas_call(
        emit_kernel,
        grid=(tokens // rows,),
        in_specs=[spec, spec, pl.BlockSpec((heads, width, width), lambda c: (0, 0, 0))],
        out_specs=pl.BlockSpec((rows, heads, width), lambda c: (c, 0, 0)),
        out_shape=jax.ShapeDtypeStruct((tokens, heads, width), BF16),
        scratch_shapes=[pltpu.VMEM((rows * heads, width), F32)],
        compiler_params=pltpu.CompilerParams(vmem_limit_bytes=VMEM_BYTES),
        cost_estimate=pl.CostEstimate(flops=10**9, bytes_accessed=8 * MIB, transcendentals=0),
        name="emit",
    )(local, probe, entry)


def finish_kernel(live, mine_ref, theirs_ref, local_ref, out_ref, rows_ref):
    slots, steps, heads, width = out_ref.shape
    for h in range(heads):
        rows_ref[pl.ds(h, steps * slots, stride=heads), :] = mine_ref[h].astype(F32) + theirs_ref[
            h
        ].astype(F32)
    on = iota2((slots, heads, width), 0) < live[0]
    for t in range(steps):
        part = rows_ref[pl.ds(t * slots * heads, slots * heads), :].reshape(slots, heads, width)
        out_ref[:, t] = jnp.where(on, part + local_ref[t], 0.0).astype(BF16)


def finish(live, mine, theirs, local):
    steps, slots, heads, width = local.shape
    return pl.pallas_call(
        finish_kernel,
        grid_spec=pltpu.PrefetchScalarGridSpec(
            num_scalar_prefetch=1,
            grid=(1,),
            in_specs=[
                pl.BlockSpec(mine.shape, lambda i, s: (0, 0, 0)),
                pl.BlockSpec(mine.shape, lambda i, s: (0, 0, 0)),
                pl.BlockSpec(local.shape, lambda i, s: (0, 0, 0, 0)),
            ],
            out_specs=pl.BlockSpec((slots, steps, heads, width), lambda i, s: (0, 0, 0, 0)),
            scratch_shapes=[pltpu.VMEM((steps * slots * heads, width), F32)],
        ),
        out_shape=jax.ShapeDtypeStruct((slots, steps, heads, width), BF16),
        compiler_params=pltpu.CompilerParams(vmem_limit_bytes=VMEM_BYTES),
        name="finish",
    )(live, mine, theirs, local)


def shifted(array, by):
    peers = lax.axis_size("dec")
    return lax.ppermute(array, "dec", [(i, i + by) for i in range(peers) if 0 <= i + by < peers])


def added(left, right):
    return (left.astype(F32) + right.astype(F32)).astype(BF16)


def local(
    prompt_query,
    prompt_key,
    prompt_value,
    prompt_beta,
    prompt_gate,
    prompt_lengths,
    request_source_prompt,
    live_counts,
    decode_query,
    decode_key,
    decode_value,
    decode_beta,
    decode_gate,
):
    peers = lax.axis_size("dec")
    tokens = prompt_query.shape[1]
    spans = tokens // SPAN
    steps = decode_query.shape[1]
    longest = peers * spans // 2
    hops = max(1, (longest - 2) // spans + 1)
    probes, decode_local = requests(decode_query, decode_key, decode_value, decode_beta, decode_gate)
    probes, prompt_key = lax.optimization_barrier((probes, prompt_key))
    all_probes = lax.all_gather(probes, ("pre", "dec"), axis=0, tiled=False)
    all_probes = all_probes.reshape((2, peers) + probes.shape)
    sources = request_source_prompt.reshape(2, peers, 1, -1)
    slots = sources.shape[3]
    sources = jnp.broadcast_to(sources, (2, peers, steps, slots)).reshape(2, peers, steps * slots, 1)

    chunk_local, chunk_probe, state, sent, own_map, table = prefill(
        prompt_lengths, prompt_query[0], prompt_key[0], prompt_value[0], prompt_beta[0], prompt_gate[0]
    )
    arrived = shifted(sent, 1) if hops > 1 else jnp.zeros_like(sent)
    next_map = shifted(own_map, -1)
    if hops > 2:
        ends = jnp.cumsum(prompt_lengths[0]) - 1
        closed = jnp.any(ends // spans == lax.axis_index("dec"))
        through = jnp.where(closed, 0.0, own_map.astype(F32)).astype(BF16)

        def turn(_, arriving):
            leaving = state + jnp.einsum("hij,hjk->hik", through, arriving, preferred_element_type=F32)
            return shifted(leaving.astype(BF16), 1)

        arrived = lax.fori_loop(0, hops - 2, turn, arrived)
    leaving, keep, send = answers(
        prompt_lengths, spans, state, own_map, arrived, next_map, table, all_probes, sources
    )
    theirs = lax.ppermute(send, "pre", [(0, 1), (1, 0)])
    block = added(keep, theirs)
    bit, part = 1, peers // 2
    while part:
        pairs = [(i, i ^ bit) for i in range(peers)]
        theirs = lax.ppermute(block[part:], "dec", pairs)
        block = block[:part]
        if bit == 1:
            entry = shifted(leaving, 1)
        if part > 1:
            block = added(block, theirs)
        bit, part = 2 * bit, part // 2
    step_result = finish(live_counts, block[0], theirs[0], decode_local)
    prompt_result = emit(chunk_local, chunk_probe, entry)[None]
    return (prompt_result, step_result)


def solution(mesh):
    in_specs = (
        P("pre", "dec", "head", None),
        P("pre", "dec", "head", None),
        P("pre", "dec", "head", None),
        P("pre", "head", "dec"),
        P("pre", "head", "dec"),
        P("pre", None),
        P(),
        P(("pre", "dec")),
        P(("pre", "dec"), None, "head", None),
        P(("pre", "dec"), None, "head", None),
        P(("pre", "dec"), None, "head", None),
        P(("pre", "dec"), None, "head"),
        P(("pre", "dec"), None, "head"),
    )
    out_specs = (P("pre", "dec", "head", None), P(("pre", "dec"), None, "head", None))
    return jax.shard_map(local, mesh=mesh, in_specs=in_specs, out_specs=out_specs, check_vma=False)
```

```python
import functools

import jax
import jax.numpy as jnp
from jax import lax
from jax.experimental import pallas as pl
from jax.experimental.pallas import tpu as pltpu
from jax.sharding import PartitionSpec as P

SPAN = 64
PROMPTS = 4
F32 = jnp.float32
BF16 = jnp.bfloat16
MIB = 1024 * 1024
VMEM_BYTES = 60 * MIB
SMALL_BYTES = 16 * MIB
EMIT_BYTES = 20 * MIB
CARRIED_MIB = 48
EMIT_ROWS = 512
BASE = 64
SUBS = 2


def dot(left, right):
    return jnp.dot(left, right, preferred_element_type=F32)


def dot_split(left, right):
    width = right.shape[1] // 2
    high = right.astype(BF16)
    low = (right[:, :width] - high[:, :width].astype(F32)).astype(BF16)
    both = dot(left, high)
    return jnp.concatenate([both[:, :width] + dot(left, low), both[:, width:]], axis=1)


def dot_last(left, right):
    return lax.dot_general(left, right, (((1,), (1,)), ((), ())), preferred_element_type=F32)


def scale_of(rows):
    return lax.rsqrt(jnp.sum(rows * rows, axis=-1, keepdims=True) + 1e-06)


def unit(rows):
    return rows * scale_of(rows)


def iota2(shape, dim):
    return lax.broadcasted_iota(jnp.int32, shape, dim)


def any_equal(marks, value):
    found = marks[0] == value
    for mark in marks[1:]:
        found = jnp.logical_or(found, mark == value)
    return found


def prompt_ends(lengths):
    ends = [lengths[0, 0] - 1]
    for j in range(1, PROMPTS):
        ends.append(ends[-1] + lengths[0, j])
    return ends


def first_end_in(ends, first, count):
    found = jnp.int32(count)
    for end in reversed(ends):
        inside = jnp.logical_and(end >= first, end < first + count)
        found = jnp.where(inside, end - first, found)
    return found


def tiled(part, size):
    return jnp.concatenate([part] * (size // part.shape[0]), axis=0)


def inverse_of(lower, masks, group):
    size = lower[0].shape[0]
    heads = range(group)
    zero = jnp.zeros((size, size), BF16)

    def packed(h, width):
        parts = [
            jnp.where(masks["lanes", width, b], lower[h][b * width : (b + 1) * width], 0.0)
            for b in range(size // width)
        ]
        return functools.reduce(lambda x, y: x + y, parts)

    def spread(part, mask):
        return jnp.where(mask, tiled(part, size), zero)

    small = [packed(h, BASE) for h in heads]
    inverse = [masks["eye"] - small[h] for h in heads]
    part = [small[h].astype(BF16) for h in heads]
    full = [spread(part[h], masks["same", BASE]) for h in heads]
    part = [dot(part[h], full[h]).astype(BF16) for h in heads]
    power = 2
    while power < BASE:
        full = [spread(part[h], masks["same", BASE]) for h in heads]
        if 2 * power < BASE:
            both = [
                dot(jnp.concatenate([part[h], inverse[h].astype(BF16)], axis=0), full[h])
                for h in heads
            ]
            part = [both[h][:BASE].astype(BF16) for h in heads]
            inverse = [inverse[h] + both[h][BASE:] for h in heads]
        else:
            inverse = [inverse[h] + dot(inverse[h].astype(BF16), full[h]) for h in heads]
        power *= 2
    inverse = [inverse[h].astype(BF16) for h in heads]
    full = [spread(inverse[h], masks["same", BASE]) for h in heads]
    width = BASE
    while width < size:
        below = []
        for h in heads:
            parts = [
                jnp.where(
                    masks["lanes", width, 2 * b],
                    lower[h][(2 * b + 1) * width : (2 * b + 2) * width],
                    0.0,
                )
                for b in range(size // (2 * width))
            ]
            below.append(functools.reduce(lambda x, y: x + y, parts).astype(BF16))
        turned = [dot(below[h], full[h]).astype(BF16) for h in heads]
        wide = [spread(turned[h], masks["off", width]) for h in heads]
        corner = [-dot(inverse[h], wide[h]) for h in heads]
        even = masks["even", width]
        corner = [corner[h].astype(BF16) for h in heads]
        inverse = [
            jnp.concatenate(
                [
                    jnp.where(even, inverse[h], jnp.zeros_like(inverse[h])),
                    jnp.where(even, corner[h], inverse[h]),
                ],
                axis=0,
            )
            for h in heads
        ]
        width *= 2
        if width < size:
            full = [spread(inverse[h], masks["same", width]) for h in heads]
    return inverse


def masks_of(size):
    row = iota2((size, size), 0)
    col = iota2((size, size), 1)
    masks = {"eye": (iota2((BASE, size), 0) == iota2((BASE, size), 1) % BASE).astype(F32)}
    width = BASE
    while width < size:
        masks["same", width] = (row // width) == (col // width)
        masks["off", width] = jnp.logical_and(
            (row // (2 * width)) == (col // (2 * width)), (row // width) != (col // width)
        )
        lanes = iota2((width, size), 1) // width
        for b in range(size // width):
            masks["lanes", width, b] = lanes == b
        masks["even", width] = lanes % 2 == 0
        width *= 2
    return masks


def chunk_kernel(
    spans,
    lengths,
    q_ref,
    k_ref,
    v_ref,
    beta_ref,
    gate_ref,
    local_ref,
    probe_ref,
    state_ref,
    first_ref,
    second_ref,
    table_ref,
    qf,
    kf,
    vf,
    walk,
    fresh,
    turned_keys,
    half_map,
    own_map,
):
    turn = pl.program_id(0)
    block_rows, heads, width = k_ref.shape
    rows = 2 * SPAN
    subs = block_rows // rows
    half = rows // 2
    places = 2 * subs

    @pl.when(turn == 0)
    def _():
        eye = (iota2((width, width), 0) == iota2((width, width), 1)).astype(F32)
        for h in range(heads):
            walk[0, h, :, :width] = jnp.zeros((width, width), F32)
            walk[0, h, :, width:] = eye
        table_ref[...] = jnp.zeros_like(table_ref)

    base = lax.axis_index("dec") * spans
    ends = [end - base for end in prompt_ends(lengths)]
    starts = [-base] + [end + 1 for end in ends[:-1]]
    map_block = jnp.minimum(first_end_in(ends, 0, spans), spans - 1)
    first_place = lax.rem(turn, 2) * subs
    first_block = 2 * subs * turn
    keeps = [
        1.0 - any_equal(starts, first_block + i).astype(F32)
        for i in range(2 * subs)
    ]

    qf[...] = q_ref[...].astype(F32).reshape(block_rows * heads, width)
    kf[...] = k_ref[...].astype(F32).reshape(block_rows * heads, width)
    vf[...] = v_ref[...].astype(F32).reshape(block_rows * heads, width)

    row = iota2((rows, rows), 0)
    col = iota2((rows, rows), 1)
    strict = row > col
    diagonal = row == col
    masks = masks_of(rows)
    lowers, row_opens, tail_opens, totals, total_cols, beta_cols = [], [], [], [], [], []
    for s in range(subs):
        keep1 = keeps[2 * s + 1]
        open_pair = jnp.logical_or(
            (row >= half) == (col >= half), jnp.full((rows, rows), keep1) > 0.5
        )
        lowers.append(jnp.logical_and(row >= col, open_pair))
        row_opens.append(jnp.where(iota2((rows, 1), 0) >= half, keep1, 1.0))
        tail_opens.append(jnp.where(iota2((rows, 1), 0) < half, keep1, 1.0))
        total = lax.dot_general(
            gate_ref[:, s * rows : (s + 1) * rows],
            (row <= col).astype(F32),
            (((1,), (0,)), ((), ())),
            precision=lax.Precision.HIGHEST,
            preferred_element_type=F32,
        )
        totals.append(total)
        total_cols.append(jnp.transpose(total))
        beta_cols.append(jnp.transpose(beta_ref[:, s * rows : (s + 1) * rows]))

    units = [(s, h) for s in range(subs) for h in range(heads)]
    idx = range(len(units))

    def rows_of(ref, s, h):
        return ref[pl.ds(s * rows * heads + h, rows, stride=heads), :]

    keys = [rows_of(kf, s, h) for s, h in units]
    queries = [rows_of(qf, s, h) for s, h in units]
    keys_half = [x.astype(BF16) for x in keys]
    queries_half = [x.astype(BF16) for x in queries]
    grams = [
        dot_last(jnp.concatenate([keys_half[i], queries_half[i]], axis=0), keys_half[i])
        for i in idx
    ]
    key_col = [scale_of(keys[i]) for i in idx]
    query_col = [scale_of(queries[i]) for i in idx]
    key_row = [
        lax.rsqrt(
            jnp.sum(jnp.where(diagonal, grams[i][:rows], 0.0), axis=0, keepdims=True) + 1e-06
        )
        for i in idx
    ]
    sums_col = [total_cols[s][:, h : h + 1] for s, h in units]
    sums_row = [totals[s][h : h + 1, :] for s, h in units]
    betas = [beta_cols[s][:, h : h + 1] for s, h in units]
    decays = [
        jnp.exp(jnp.where(lowers[units[i][0]], sums_col[i] - sums_row[i], -1e30)) * key_row[i]
        for i in idx
    ]
    strict_part = [
        jnp.where(strict, (betas[i] * key_col[i]) * (decays[i] * grams[i][:rows]), 0.0)
        for i in idx
    ]
    scores = [(query_col[i] * (decays[i] * grams[i][rows:])).astype(BF16) for i in idx]
    growth = [jnp.exp(sums_col[i]) * row_opens[units[i][0]] for i in idx]
    inverse = inverse_of(strict_part, masks, len(units))
    right = [
        jnp.concatenate(
            [
                (keys[i] * (betas[i] * growth[i] * key_col[i])).astype(BF16),
                (rows_of(vf, *units[i]) * betas[i]).astype(BF16),
            ],
            axis=1,
        )
        for i in idx
    ]
    wu = [dot(inverse[i], right[i]) for i in idx]
    turned = [jnp.transpose(keys_half[i]) for i in idx]
    tails = [
        jnp.exp(sums_row[i][:, rows - 1 :] - sums_col[i]) * (key_col[i] * tail_opens[units[i][0]])
        for i in idx
    ]
    grown = [(queries[i] * (growth[i] * query_col[i])).astype(BF16) for i in idx]
    entry = [walk[first_place, h] for h in range(heads)]
    for s in range(subs):
        mine = [s * heads + h for h in range(heads)]
        entry = [x * keeps[2 * s] for x in entry]
        entry_half = [x.astype(BF16) for x in entry]
        moved = [dot(wu[i][:, :width].astype(BF16), entry_half[i % heads]) for i in mine]
        new = [
            jnp.concatenate(
                [
                    wu[i][:, width:] - moved[i % heads][:, :width],
                    -moved[i % heads][:, width:],
                ],
                axis=1,
            )
            for i in mine
        ]
        for h in range(heads):
            fresh[s, h] = new[h]
        leaving = [
            entry[i % heads] * (jnp.exp(sums_row[i][:, rows - 1 :]) * keeps[2 * s + 1])
            + dot_split(turned[i], new[i % heads] * tails[i])
            for i in mine
        ]
        new = [x.astype(BF16) for x in new]
        outs = [
            dot(
                jnp.concatenate([grown[i], scores[i]], axis=1),
                jnp.concatenate([entry_half[i % heads], new[i % heads]], axis=0),
            )
            for i in mine
        ]
        place = lax.rem(first_place + s + 1, places)
        for h in range(heads):
            walk[place, h] = leaving[h]
            turned_keys[s, h] = turned[mine[h]]
            local_ref[h, s * rows : (s + 1) * rows] = outs[h][:, :width]
            probe_ref[h, s * rows : (s + 1) * rows] = outs[h][:, width:].astype(BF16)
        entry = leaving

    for s in range(subs):
        block0 = first_block + 2 * s
        now = lax.rem(first_place + s, places)
        later = lax.rem(first_place + s + 1, places)

        @pl.when(any_equal(ends, block0))
        def _(s=s, block0=block0, now=now):
            prompt = jnp.int32(0)
            for j in range(1, PROMPTS):
                prompt = jnp.where(ends[j] == block0, j, prompt)
            at_half = [totals[s][h : h + 1, half - 1 : half] for h in range(heads)]
            first_half = iota2((rows, 1), 0) < half
            weights = [
                jnp.exp(jnp.where(first_half, at_half[h] - total_cols[s][:, h : h + 1], -1e30))
                for h in range(heads)
            ]
            weights = [weights[h] * scale_of(rows_of(kf, s, h)) for h in range(heads)]
            steps = [dot_split(turned_keys[s, h], fresh[s, h] * weights[h]) for h in range(heads)]
            for h in range(heads):
                state = walk[now, h] * (keeps[2 * s] * jnp.exp(at_half[h])) + steps[h]
                table_ref[prompt, h] = state[:, :width].astype(BF16)
                half_map[h] = state[:, width:].astype(BF16)

            @pl.when(map_block == block0)
            def _():
                own_map[...] = half_map[...]

        for j in range(PROMPTS):

            @pl.when(ends[j] == block0 + 1)
            def _(j=j, later=later):
                table_ref[j] = walk[later, :, :, :width].astype(BF16)

        @pl.when(map_block == block0 + 1)
        def _(later=later):
            own_map[...] = walk[later, :, :, width:].astype(BF16)

    @pl.when(turn == pl.num_programs(0) - 1)
    def _():
        last = walk[lax.rem(first_place + subs, places), :, :, :width]
        state_ref[...] = last
        odd = jnp.full(last.shape, lax.rem(lax.axis_index("dec"), 2)) == 1
        first_ref[...] = jnp.where(odd, own_map[...], last.astype(BF16))
        second_ref[...] = jnp.where(odd, last.astype(BF16), own_map[...])


def prefill(lengths, query, key, value, beta, gate):
    tokens, heads, width = key.shape
    rows = 2 * SPAN * SUBS
    token_spec = pl.BlockSpec((rows, heads, width), lambda c, s: (c, 0, 0))
    gate_spec = pl.BlockSpec((heads, rows), lambda c, s: (0, c))
    out_spec = pl.BlockSpec((heads, rows, width), lambda c, s: (0, c, 0))
    whole = pl.BlockSpec((heads, width, width), lambda c, s: (0, 0, 0))
    table_spec = pl.BlockSpec((PROMPTS, heads, width, width), lambda c, s: (0, 0, 0, 0))
    return pl.pallas_call(
        functools.partial(chunk_kernel, tokens // SPAN),
        grid_spec=pltpu.PrefetchScalarGridSpec(
            num_scalar_prefetch=1,
            grid=(tokens // rows,),
            in_specs=[token_spec, token_spec, token_spec, gate_spec, gate_spec],
            out_specs=[out_spec, out_spec, whole, whole, whole, table_spec],
            scratch_shapes=[
                pltpu.VMEM((rows * heads, width), F32),
                pltpu.VMEM((rows * heads, width), F32),
                pltpu.VMEM((rows * heads, width), F32),
                pltpu.VMEM((2 * SUBS, heads, width, 2 * width), F32),
                pltpu.VMEM((SUBS, heads, 2 * SPAN, 2 * width), F32),
                pltpu.VMEM((SUBS, heads, width, 2 * SPAN), BF16),
                pltpu.VMEM((heads, width, width), BF16),
                pltpu.VMEM((heads, width, width), BF16),
            ],
        ),
        out_shape=[
            jax.ShapeDtypeStruct((heads, tokens, width), F32),
            jax.ShapeDtypeStruct((heads, tokens, width), BF16),
            jax.ShapeDtypeStruct((heads, width, width), F32),
            jax.ShapeDtypeStruct((heads, width, width), BF16),
            jax.ShapeDtypeStruct((heads, width, width), BF16),
            jax.ShapeDtypeStruct((PROMPTS, heads, width, width), BF16),
        ],
        compiler_params=pltpu.CompilerParams(vmem_limit_bytes=VMEM_BYTES),
        cost_estimate=pl.CostEstimate(flops=6 * 10**9, bytes_accessed=16 * MIB, transcendentals=0),
        name="chunks",
    )(lengths, query, key, value, beta, gate)


def request_kernel(q_ref, k_ref, v_ref, beta_ref, gate_ref, probe_ref, local_ref, rows_ref):
    slots, steps, heads, width = q_ref.shape

    def per_slot(ref, t):
        values = ref[t].astype(F32)
        return jnp.stack(
            [jnp.broadcast_to(values[:, i : i + 1], (heads, width)) for i in range(slots)]
        )

    keys = [unit(k_ref[:, t].astype(F32)) for t in range(steps)]
    queries = [unit(q_ref[:, t].astype(F32)) for t in range(steps)]
    gates = []
    for t in range(steps):
        gate = per_slot(gate_ref, t)
        gates.append(gate if t == 0 else gates[-1] + gate)
    weights, updates = [], []
    for t in range(steps):
        beta = per_slot(beta_ref, t)
        reach = jnp.exp(gates[t]) * keys[t]
        value = v_ref[:, t].astype(F32)
        for s in range(t):
            factor = jnp.exp(gates[t] - gates[s]) * jnp.sum(keys[s] * keys[t], axis=-1, keepdims=True)
            reach = reach - factor * weights[s]
            value = value - factor * updates[s]
        weights.append(beta * reach)
        updates.append(beta * value)
        probe = jnp.exp(gates[t]) * queries[t]
        emitted = jnp.zeros_like(value)
        for s in range(t + 1):
            factor = jnp.sum(keys[s] * queries[t], axis=-1, keepdims=True)
            factor = factor if s == t else factor * jnp.exp(gates[t] - gates[s])
            probe = probe - factor * weights[s]
            emitted = emitted + factor * updates[s]
        rows_ref[pl.ds(t * slots * heads, slots * heads), :] = probe.reshape(slots * heads, width)
        local_ref[t] = emitted
    for h in range(heads):
        probe_ref[h] = rows_ref[pl.ds(h, steps * slots, stride=heads), :].astype(BF16)


def requests(query, key, value, beta, gate):
    slots, steps, heads, width = query.shape
    beta, gate = jnp.transpose(beta, (1, 2, 0)), jnp.transpose(gate, (1, 2, 0))
    return pl.pallas_call(
        request_kernel,
        out_shape=[
            jax.ShapeDtypeStruct((heads, steps * slots, width), BF16),
            jax.ShapeDtypeStruct((steps, slots, heads, width), F32),
        ],
        scratch_shapes=[pltpu.VMEM((steps * slots * heads, width), F32)],
        compiler_params=pltpu.CompilerParams(vmem_limit_bytes=VMEM_BYTES),
        name="requests",
    )(query, key, value, beta, gate)


def reversed_bits(value, count):
    bits, turned = count.bit_length() - 1, 0
    for i in range(bits):
        turned |= ((value >> i) & 1) << (bits - 1 - i)
    return turned


def reversed_bits(value, count):
    bits, turned = count.bit_length() - 1, 0
    for i in range(bits):
        turned |= ((value >> i) & 1) << (bits - 1 - i)
    return turned


def spread_sources(source_ref, out_ref):
    _, peers, rows, _ = source_ref.shape
    me, mine = lax.axis_index("dec"), lax.axis_index("pre")
    for p in range(2):
        for x in range(peers):
            first = (p * peers + x) * rows
            peer = jnp.bitwise_xor(me, reversed_bits(x, peers))
            out_ref[first : first + rows, :] = jnp.broadcast_to(
                source_ref[lax.rem(mine + p, 2), peer], (rows, out_ref.shape[1])
            )


def stored_kernel(spans, lengths, table_ref, own_ref, other_ref, source_ref, keep_ref, send_ref, source_rows, total):
    peers, _, rows, width = own_ref.shape
    mine = lax.axis_index("pre")
    ends = prompt_ends(lengths)
    base = lax.axis_index("dec") * spans
    size = peers * rows

    @pl.when(pl.program_id(0) == 0)
    def _():
        spread_sources(source_ref, source_rows)

    total[...] = jnp.zeros_like(total)
    for j in range(PROMPTS):

        @pl.when(jnp.logical_and(ends[j] >= base, ends[j] < base + spans))
        def _(j=j):
            for first, ref in ((0, own_ref), (size, other_ref)):
                rows_here = slice(first, first + size)
                total[rows_here] = jnp.where(
                    source_rows[rows_here] == mine * PROMPTS + j,
                    dot(ref[:, 0].reshape(size, width), table_ref[j, 0]),
                    total[rows_here],
                )

    keep_ref[:, 0] = total[:size].astype(BF16).reshape(peers, rows, width)
    send_ref[:, 0] = total[size:].astype(BF16).reshape(peers, rows, width)


def stored_answers(lengths, spans, table, own, other, sources):
    peers, heads, rows, width = own.shape
    table_spec = pl.BlockSpec((PROMPTS, 1, width, width), lambda h, s: (0, h, 0, 0))
    rows_spec = pl.BlockSpec((peers, 1, rows, width), lambda h, s: (0, h, 0, 0))
    source_spec = pl.BlockSpec((2, peers, rows, 1), lambda h, s: (0, 0, 0, 0))
    out = jax.ShapeDtypeStruct(own.shape, BF16)
    return pl.pallas_call(
        functools.partial(stored_kernel, spans),
        grid_spec=pltpu.PrefetchScalarGridSpec(
            num_scalar_prefetch=1,
            grid=(heads,),
            in_specs=[table_spec, rows_spec, rows_spec, source_spec],
            out_specs=[rows_spec, rows_spec],
            scratch_shapes=[
                pltpu.VMEM((2 * peers * rows, width), jnp.int32),
                pltpu.VMEM((2 * peers * rows, width), F32),
            ],
        ),
        out_shape=[out, out],
        compiler_params=pltpu.CompilerParams(vmem_limit_bytes=16 * MIB),
        cost_estimate=pl.CostEstimate(flops=10**9, bytes_accessed=16 * MIB, transcendentals=0),
        name="stored",
    )(lengths, table, own, other, sources)


def carried_kernel(
    spans,
    lengths,
    state_ref,
    first_ref,
    second_ref,
    first_got_ref,
    second_got_ref,
    own_ref,
    other_ref,
    own_part_ref,
    other_part_ref,
    source_ref,
    sent_ref,
    keep_ref,
    send_ref,
    source_rows,
):
    peers, heads, rows, width = own_ref.shape
    mine = lax.axis_index("pre")
    ends = prompt_ends(lengths)
    base = lax.axis_index("dec") * spans
    size = peers * rows
    through = jnp.where(first_end_in(ends, base, spans) < spans, 0.0, 1.0)
    next_end = base + spans + first_end_in(ends, base + spans, spans)
    next_prompt = jnp.int32(-1)
    for j in range(PROMPTS):
        next_prompt = jnp.where(ends[j] == next_end, mine * PROMPTS + j, next_prompt)
    spread_sources(source_ref, source_rows)
    odd = jnp.full((width, width), lax.rem(lax.axis_index("dec"), 2)) == 1
    leaving, carried = [], []
    for h in range(heads):
        own_map = jnp.where(odd, first_ref[h], second_ref[h])
        arrived = jnp.where(odd, first_got_ref[h], second_got_ref[h])
        leaving.append((state_ref[h] + through * dot(own_map, arrived)).astype(BF16))
    for h in range(heads):
        next_map = jnp.where(odd, second_got_ref[h], first_got_ref[h])
        carried.append(dot(next_map, leaving[h]).astype(BF16))
    for h in range(heads):
        sent_ref[h] = leaving[h]
        for first, ref, part, out in (
            (0, own_ref, own_part_ref, keep_ref),
            (size, other_ref, other_part_ref, send_ref),
        ):
            out[:, h] = (
                jnp.where(
                    source_rows[first : first + size] == next_prompt,
                    dot(ref[:, h].reshape(size, width), carried[h]),
                    part[:, h].reshape(size, width).astype(F32),
                )
                .astype(BF16)
                .reshape(peers, rows, width)
            )


def carried_answers(lengths, spans, state, first, second, own, other, own_part, other_part, sources):
    peers, heads, rows, width = own.shape
    out = jax.ShapeDtypeStruct(own.shape, BF16)
    return pl.pallas_call(
        functools.partial(carried_kernel, spans),
        grid_spec=pltpu.PrefetchScalarGridSpec(
            num_scalar_prefetch=1,
            grid=(1,),
            in_specs=[pl.BlockSpec(memory_space=pltpu.VMEM)] * 10,
            out_specs=[pl.BlockSpec(memory_space=pltpu.VMEM)] * 3,
            scratch_shapes=[pltpu.VMEM((2 * peers * rows, width), jnp.int32)],
        ),
        out_shape=[jax.ShapeDtypeStruct((heads, width, width), BF16), out, out],
        compiler_params=pltpu.CompilerParams(vmem_limit_bytes=CARRIED_MIB * MIB),
        name="carried",
    )(lengths, state, first[0], second[0], first[1], second[1], own, other, own_part, other_part, sources)


def emit_kernel(local_ref, probe_ref, entry_ref, out_ref, rows_ref):
    heads, rows, width = local_ref.shape
    for h in range(heads):
        rows_ref[pl.ds(h, rows, stride=heads), :] = local_ref[h] + dot(probe_ref[h], entry_ref[h])
    out_ref[...] = rows_ref[...].reshape(rows, heads, width).astype(BF16)


def emit(local, probe, entry):
    heads, tokens, width = local.shape
    rows = EMIT_ROWS
    spec = pl.BlockSpec((heads, rows, width), lambda c: (0, c, 0))
    return pl.pallas_call(
        emit_kernel,
        grid=(tokens // rows,),
        in_specs=[spec, spec, pl.BlockSpec((heads, width, width), lambda c: (0, 0, 0))],
        out_specs=pl.BlockSpec((rows, heads, width), lambda c: (c, 0, 0)),
        out_shape=jax.ShapeDtypeStruct((tokens, heads, width), BF16),
        scratch_shapes=[pltpu.VMEM((rows * heads, width), F32)],
        compiler_params=pltpu.CompilerParams(vmem_limit_bytes=EMIT_BYTES),
        cost_estimate=pl.CostEstimate(flops=10**9, bytes_accessed=8 * MIB, transcendentals=0),
        name="emit",
    )(local, probe, entry)


def finish_kernel(live, mine_ref, near_ref, far_ref, local_ref, out_ref, rows_ref):
    slots, steps, heads, width = out_ref.shape
    for h in range(heads):
        rows_ref[pl.ds(h, steps * slots, stride=heads), :] = (
            mine_ref[0, h].astype(F32) + near_ref[0, h].astype(F32)
        ) + far_ref[0, h].astype(F32)
    on = iota2((slots, heads, width), 0) < live[0]
    for t in range(steps):
        part = rows_ref[pl.ds(t * slots * heads, slots * heads), :].reshape(slots, heads, width)
        out_ref[:, t] = jnp.where(on, part + local_ref[t], 0.0).astype(BF16)


def finish(live, mine, near, far, local):
    steps, slots, heads, width = local.shape
    return pl.pallas_call(
        finish_kernel,
        grid_spec=pltpu.PrefetchScalarGridSpec(
            num_scalar_prefetch=1,
            grid=(1,),
            in_specs=[
                pl.BlockSpec((1,) + mine.shape[1:], lambda i, s: (0, 0, 0, 0)),
                pl.BlockSpec((1,) + near.shape[1:], lambda i, s: (0, 0, 0, 0)),
                pl.BlockSpec((1,) + far.shape[1:], lambda i, s: (0, 0, 0, 0)),
                pl.BlockSpec(local.shape, lambda i, s: (0, 0, 0, 0)),
            ],
            out_specs=pl.BlockSpec((slots, steps, heads, width), lambda i, s: (0, 0, 0, 0)),
            scratch_shapes=[pltpu.VMEM((steps * slots * heads, width), F32)],
        ),
        out_shape=jax.ShapeDtypeStruct((slots, steps, heads, width), BF16),
        compiler_params=pltpu.CompilerParams(vmem_limit_bytes=SMALL_BYTES),
        name="finish",
    )(live, mine, near, far, local)


def shifted(array, by):
    peers = lax.axis_size("dec")
    return lax.ppermute(array, "dec", [(i, i + by) for i in range(peers) if 0 <= i + by < peers])


def added(left, right):
    return (left.astype(F32) + right.astype(F32)).astype(BF16)


def local(
    prompt_query,
    prompt_key,
    prompt_value,
    prompt_beta,
    prompt_gate,
    prompt_lengths,
    request_source_prompt,
    live_counts,
    decode_query,
    decode_key,
    decode_value,
    decode_beta,
    decode_gate,
):
    peers = lax.axis_size("dec")
    tokens = prompt_query.shape[1]
    spans = tokens // SPAN
    steps = decode_query.shape[1]
    longest = peers * spans // 2
    hops = max(1, (longest - 2) // spans + 1)
    probes, decode_local = requests(decode_query, decode_key, decode_value, decode_beta, decode_gate)
    own_probes = [probes]
    for x in range(1, peers):
        pairs = [(i, i ^ reversed_bits(x, peers)) for i in range(peers)]
        own_probes.append(lax.ppermute(probes, "dec", pairs))
    probes, prompt_key = lax.optimization_barrier((probes, prompt_key))
    sources = request_source_prompt.reshape(2, peers, 1, -1)
    slots = sources.shape[3]
    sources = jnp.broadcast_to(sources, (2, peers, steps, slots)).reshape(2, peers, steps * slots, 1)

    chunk_local, chunk_probe, state, first, second, table = prefill(
        prompt_lengths, prompt_query[0], prompt_key[0], prompt_value[0], prompt_beta[0], prompt_gate[0]
    )
    own_probes, first, second = lax.optimization_barrier((own_probes, first, second))
    pairs = [(i, i ^ 1) for i in range(peers)]
    first_got = lax.ppermute(first, "dec", pairs)
    pairs = [(i, (i + 1 ^ 1) - 1) for i in range(1, peers - 1)]
    second_got = lax.ppermute(second, "dec", pairs)
    if hops > 2:
        odd = lax.axis_index("dec") % 2 == 1
        ends = jnp.cumsum(prompt_lengths[0]) - 1
        closed = jnp.any(ends // spans == lax.axis_index("dec"))
        own_map = jnp.where(odd, first, second)
        through = jnp.where(closed, 0.0, own_map.astype(F32)).astype(BF16)

        def turn(_, arriving):
            leaving = state + jnp.einsum("hij,hjk->hik", through, arriving, preferred_element_type=F32)
            return shifted(leaving.astype(BF16), 1)

        arrived = lax.fori_loop(0, hops - 2, turn, jnp.where(odd, first_got, second_got))
        first_got, second_got = (
            jnp.where(odd, arrived, first_got),
            jnp.where(odd, second_got, arrived),
        )
    own_probes = jnp.stack(own_probes)
    other_probes = lax.ppermute(own_probes, "pre", [(0, 1), (1, 0)])
    own_part, other_part = stored_answers(prompt_lengths, spans, table, own_probes, other_probes, sources)
    leaving, keep, send = carried_answers(
        prompt_lengths,
        spans,
        state,
        (first, first_got),
        (second, second_got),
        own_probes,
        other_probes,
        own_part,
        other_part,
        sources,
    )
    theirs = lax.ppermute(send, "pre", [(0, 1), (1, 0)])
    entry = shifted(leaving, 1)
    block = added(keep, theirs)
    theirs = jnp.zeros_like(block)
    bit, part = 1, peers // 2
    while part:
        pairs = [(i, i ^ bit) for i in range(peers)]
        if bit == 1:
            outgoing = block[part:]
        else:
            outgoing = added(block[part : 2 * part], theirs[part : 2 * part])
        if bit > 1 and part > 1:
            block = added(block[:part], theirs[:part])
        before, theirs = theirs, lax.ppermute(outgoing, "dec", pairs)
        bit, part = 2 * bit, part // 2
    step_result = finish(live_counts, block, before, theirs, decode_local)
    prompt_result = emit(chunk_local, chunk_probe, entry)[None]
    return (prompt_result, step_result)


def solution(mesh):
    in_specs = (
        P("pre", "dec", "head", None),
        P("pre", "dec", "head", None),
        P("pre", "dec", "head", None),
        P("pre", "head", "dec"),
        P("pre", "head", "dec"),
        P("pre", None),
        P(),
        P(("pre", "dec")),
        P(("pre", "dec"), None, "head", None),
        P(("pre", "dec"), None, "head", None),
        P(("pre", "dec"), None, "head", None),
        P(("pre", "dec"), None, "head"),
        P(("pre", "dec"), None, "head"),
    )
    out_specs = (P("pre", "dec", "head", None), P(("pre", "dec"), None, "head", None))
    return jax.shard_map(local, mesh=mesh, in_specs=in_specs, out_specs=out_specs, check_vma=False)
```

```python
import functools

import jax
import jax.numpy as jnp
from jax import lax
from jax.experimental import pallas as pl
from jax.experimental.pallas import tpu as pltpu
from jax.sharding import PartitionSpec as P

SPAN = 64
PROMPTS = 4
F32 = jnp.float32
BF16 = jnp.bfloat16
MIB = 1024 * 1024
VMEM_BYTES = 60 * MIB
SMALL_BYTES = 16 * MIB
EMIT_BYTES = 20 * MIB
CARRIED_MIB = 48
EMIT_ROWS = 512
BASE = 64
SUBS = 2


def dot(left, right):
    return jnp.dot(left, right, preferred_element_type=F32)


def dot_split(left, right):
    width = right.shape[1] // 2
    high = right.astype(BF16)
    low = (right[:, :width] - high[:, :width].astype(F32)).astype(BF16)
    both = dot(left, high)
    return jnp.concatenate([both[:, :width] + dot(left, low), both[:, width:]], axis=1)


def dot_last(left, right):
    return lax.dot_general(left, right, (((1,), (1,)), ((), ())), preferred_element_type=F32)


def scale_of(rows):
    return lax.rsqrt(jnp.sum(rows * rows, axis=-1, keepdims=True) + 1e-06)


def unit(rows):
    return rows * scale_of(rows)


def iota2(shape, dim):
    return lax.broadcasted_iota(jnp.int32, shape, dim)


def any_equal(marks, value):
    found = marks[0] == value
    for mark in marks[1:]:
        found = jnp.logical_or(found, mark == value)
    return found


def prompt_ends(lengths):
    ends = [lengths[0, 0] - 1]
    for j in range(1, PROMPTS):
        ends.append(ends[-1] + lengths[0, j])
    return ends


def first_end_in(ends, first, count):
    found = jnp.int32(count)
    for end in reversed(ends):
        inside = jnp.logical_and(end >= first, end < first + count)
        found = jnp.where(inside, end - first, found)
    return found


def tiled(part, size):
    return jnp.concatenate([part] * (size // part.shape[0]), axis=0)


def inverse_of(lower, masks, group):
    size = lower[0].shape[0]
    heads = range(group)
    zero = jnp.zeros((size, size), BF16)

    def packed(h, width):
        parts = [
            jnp.where(masks["lanes", width, b], lower[h][b * width : (b + 1) * width], 0.0)
            for b in range(size // width)
        ]
        return functools.reduce(lambda x, y: x + y, parts)

    def spread(part, mask):
        return jnp.where(mask, tiled(part, size), zero)

    small = [packed(h, BASE) for h in heads]
    inverse = [masks["eye"] - small[h] for h in heads]
    part = [small[h].astype(BF16) for h in heads]
    full = [spread(part[h], masks["same", BASE]) for h in heads]
    part = [dot(part[h], full[h]).astype(BF16) for h in heads]
    power = 2
    while power < BASE:
        full = [spread(part[h], masks["same", BASE]) for h in heads]
        if 2 * power < BASE:
            both = [
                dot(jnp.concatenate([part[h], inverse[h].astype(BF16)], axis=0), full[h])
                for h in heads
            ]
            part = [both[h][:BASE].astype(BF16) for h in heads]
            inverse = [inverse[h] + both[h][BASE:] for h in heads]
        else:
            inverse = [inverse[h] + dot(inverse[h].astype(BF16), full[h]) for h in heads]
        power *= 2
    inverse = [inverse[h].astype(BF16) for h in heads]
    full = [spread(inverse[h], masks["same", BASE]) for h in heads]
    width = BASE
    while width < size:
        below = []
        for h in heads:
            parts = [
                jnp.where(
                    masks["lanes", width, 2 * b],
                    lower[h][(2 * b + 1) * width : (2 * b + 2) * width],
                    0.0,
                )
                for b in range(size // (2 * width))
            ]
            below.append(functools.reduce(lambda x, y: x + y, parts).astype(BF16))
        turned = [dot(below[h], full[h]).astype(BF16) for h in heads]
        wide = [spread(turned[h], masks["off", width]) for h in heads]
        corner = [-dot(inverse[h], wide[h]) for h in heads]
        even = masks["even", width]
        corner = [corner[h].astype(BF16) for h in heads]
        inverse = [
            jnp.concatenate(
                [
                    jnp.where(even, inverse[h], jnp.zeros_like(inverse[h])),
                    jnp.where(even, corner[h], inverse[h]),
                ],
                axis=0,
            )
            for h in heads
        ]
        width *= 2
        if width < size:
            full = [spread(inverse[h], masks["same", width]) for h in heads]
    return inverse


def masks_of(size):
    row = iota2((size, size), 0)
    col = iota2((size, size), 1)
    masks = {"eye": (iota2((BASE, size), 0) == iota2((BASE, size), 1) % BASE).astype(F32)}
    width = BASE
    while width < size:
        masks["same", width] = (row // width) == (col // width)
        masks["off", width] = jnp.logical_and(
            (row // (2 * width)) == (col // (2 * width)), (row // width) != (col // width)
        )
        lanes = iota2((width, size), 1) // width
        for b in range(size // width):
            masks["lanes", width, b] = lanes == b
        masks["even", width] = lanes % 2 == 0
        width *= 2
    return masks


def chunk_kernel(
    spans,
    lengths,
    q_ref,
    k_ref,
    v_ref,
    beta_ref,
    gate_ref,
    local_ref,
    probe_ref,
    state_ref,
    first_ref,
    second_ref,
    table_ref,
    qf,
    kf,
    vf,
    walk,
    fresh,
    turned_keys,
    half_map,
    own_map,
):
    turn = pl.program_id(0)
    block_rows, heads, width = k_ref.shape
    rows = 2 * SPAN
    subs = block_rows // rows
    half = rows // 2
    places = 2 * subs

    @pl.when(turn == 0)
    def _():
        eye = (iota2((width, width), 0) == iota2((width, width), 1)).astype(F32)
        for h in range(heads):
            walk[0, h, :, :width] = jnp.zeros((width, width), F32)
            walk[0, h, :, width:] = eye
        table_ref[...] = jnp.zeros_like(table_ref)

    base = lax.axis_index("dec") * spans
    ends = [end - base for end in prompt_ends(lengths)]
    starts = [-base] + [end + 1 for end in ends[:-1]]
    map_block = jnp.minimum(first_end_in(ends, 0, spans), spans - 1)
    first_place = lax.rem(turn, 2) * subs
    first_block = 2 * subs * turn
    keeps = [
        1.0 - any_equal(starts, first_block + i).astype(F32)
        for i in range(2 * subs)
    ]

    qf[...] = q_ref[...].astype(F32).reshape(block_rows * heads, width)
    kf[...] = k_ref[...].astype(F32).reshape(block_rows * heads, width)
    vf[...] = v_ref[...].astype(F32).reshape(block_rows * heads, width)

    row = iota2((rows, rows), 0)
    col = iota2((rows, rows), 1)
    strict = row > col
    diagonal = row == col
    masks = masks_of(rows)
    lowers, row_opens, tail_opens, totals, total_cols, beta_cols = [], [], [], [], [], []
    for s in range(subs):
        keep1 = keeps[2 * s + 1]
        open_pair = jnp.logical_or(
            (row >= half) == (col >= half), jnp.full((rows, rows), keep1) > 0.5
        )
        lowers.append(jnp.logical_and(row >= col, open_pair))
        row_opens.append(jnp.where(iota2((rows, 1), 0) >= half, keep1, 1.0))
        tail_opens.append(jnp.where(iota2((rows, 1), 0) < half, keep1, 1.0))
        total = lax.dot_general(
            gate_ref[:, s * rows : (s + 1) * rows],
            (row <= col).astype(F32),
            (((1,), (0,)), ((), ())),
            precision=lax.Precision.HIGHEST,
            preferred_element_type=F32,
        )
        totals.append(total)
        total_cols.append(jnp.transpose(total))
        beta_cols.append(jnp.transpose(beta_ref[:, s * rows : (s + 1) * rows]))

    units = [(s, h) for s in range(subs) for h in range(heads)]
    idx = range(len(units))

    def rows_of(ref, s, h):
        return ref[pl.ds(s * rows * heads + h, rows, stride=heads), :]

    keys = [rows_of(kf, s, h) for s, h in units]
    queries = [rows_of(qf, s, h) for s, h in units]
    keys_half = [x.astype(BF16) for x in keys]
    queries_half = [x.astype(BF16) for x in queries]
    grams = [
        dot_last(jnp.concatenate([keys_half[i], queries_half[i]], axis=0), keys_half[i])
        for i in idx
    ]
    key_col = [scale_of(keys[i]) for i in idx]
    query_col = [scale_of(queries[i]) for i in idx]
    key_row = [
        lax.rsqrt(
            jnp.sum(jnp.where(diagonal, grams[i][:rows], 0.0), axis=0, keepdims=True) + 1e-06
        )
        for i in idx
    ]
    sums_col = [total_cols[s][:, h : h + 1] for s, h in units]
    sums_row = [totals[s][h : h + 1, :] for s, h in units]
    betas = [beta_cols[s][:, h : h + 1] for s, h in units]
    decays = [
        jnp.exp(jnp.where(lowers[units[i][0]], sums_col[i] - sums_row[i], -1e30)) * key_row[i]
        for i in idx
    ]
    strict_part = [
        jnp.where(strict, (betas[i] * key_col[i]) * (decays[i] * grams[i][:rows]), 0.0)
        for i in idx
    ]
    scores = [(query_col[i] * (decays[i] * grams[i][rows:])).astype(BF16) for i in idx]
    growth = [jnp.exp(sums_col[i]) * row_opens[units[i][0]] for i in idx]
    inverse = inverse_of(strict_part, masks, len(units))
    right = [
        jnp.concatenate(
            [
                (keys[i] * (betas[i] * growth[i] * key_col[i])).astype(BF16),
                (rows_of(vf, *units[i]) * betas[i]).astype(BF16),
            ],
            axis=1,
        )
        for i in idx
    ]
    wu = [dot(inverse[i], right[i]) for i in idx]
    turned = [jnp.transpose(keys_half[i]) for i in idx]
    tails = [
        jnp.exp(sums_row[i][:, rows - 1 :] - sums_col[i]) * (key_col[i] * tail_opens[units[i][0]])
        for i in idx
    ]
    grown = [(queries[i] * (growth[i] * query_col[i])).astype(BF16) for i in idx]
    entry = [walk[first_place, h] for h in range(heads)]
    for s in range(subs):
        mine = [s * heads + h for h in range(heads)]
        entry = [x * keeps[2 * s] for x in entry]
        entry_half = [x.astype(BF16) for x in entry]
        moved = [dot(wu[i][:, :width].astype(BF16), entry_half[i % heads]) for i in mine]
        new = [
            jnp.concatenate(
                [
                    wu[i][:, width:] - moved[i % heads][:, :width],
                    -moved[i % heads][:, width:],
                ],
                axis=1,
            )
            for i in mine
        ]
        for h in range(heads):
            fresh[s, h] = new[h]
        leaving = [
            entry[i % heads] * (jnp.exp(sums_row[i][:, rows - 1 :]) * keeps[2 * s + 1])
            + dot_split(turned[i], new[i % heads] * tails[i])
            for i in mine
        ]
        new = [x.astype(BF16) for x in new]
        outs = [
            dot(
                jnp.concatenate([grown[i], scores[i]], axis=1),
                jnp.concatenate([entry_half[i % heads], new[i % heads]], axis=0),
            )
            for i in mine
        ]
        place = lax.rem(first_place + s + 1, places)
        for h in range(heads):
            walk[place, h] = leaving[h]
            turned_keys[s, h] = turned[mine[h]]
            local_ref[h, s * rows : (s + 1) * rows] = outs[h][:, :width]
            probe_ref[h, s * rows : (s + 1) * rows] = outs[h][:, width:].astype(BF16)
        entry = leaving

    for s in range(subs):
        block0 = first_block + 2 * s
        now = lax.rem(first_place + s, places)
        later = lax.rem(first_place + s + 1, places)

        @pl.when(any_equal(ends, block0))
        def _(s=s, block0=block0, now=now):
            prompt = jnp.int32(0)
            for j in range(1, PROMPTS):
                prompt = jnp.where(ends[j] == block0, j, prompt)
            at_half = [totals[s][h : h + 1, half - 1 : half] for h in range(heads)]
            first_half = iota2((rows, 1), 0) < half
            weights = [
                jnp.exp(jnp.where(first_half, at_half[h] - total_cols[s][:, h : h + 1], -1e30))
                for h in range(heads)
            ]
            weights = [weights[h] * scale_of(rows_of(kf, s, h)) for h in range(heads)]
            steps = [dot_split(turned_keys[s, h], fresh[s, h] * weights[h]) for h in range(heads)]
            for h in range(heads):
                state = walk[now, h] * (keeps[2 * s] * jnp.exp(at_half[h])) + steps[h]
                table_ref[prompt, h] = state[:, :width].astype(BF16)
                half_map[h] = state[:, width:].astype(BF16)

            @pl.when(map_block == block0)
            def _():
                own_map[...] = half_map[...]

        for j in range(PROMPTS):

            @pl.when(ends[j] == block0 + 1)
            def _(j=j, later=later):
                table_ref[j] = walk[later, :, :, :width].astype(BF16)

        @pl.when(map_block == block0 + 1)
        def _(later=later):
            own_map[...] = walk[later, :, :, width:].astype(BF16)

    @pl.when(turn == pl.num_programs(0) - 1)
    def _():
        last = walk[lax.rem(first_place + subs, places), :, :, :width]
        state_ref[...] = last
        odd = jnp.full(last.shape, lax.rem(lax.axis_index("dec"), 2)) == 1
        first_ref[...] = jnp.where(odd, own_map[...], last.astype(BF16))
        second_ref[...] = jnp.where(odd, last.astype(BF16), own_map[...])


def prefill(lengths, query, key, value, beta, gate):
    tokens, heads, width = key.shape
    rows = 2 * SPAN * SUBS
    token_spec = pl.BlockSpec((rows, heads, width), lambda c, s: (c, 0, 0))
    gate_spec = pl.BlockSpec((heads, rows), lambda c, s: (0, c))
    out_spec = pl.BlockSpec((heads, rows, width), lambda c, s: (0, c, 0))
    whole = pl.BlockSpec((heads, width, width), lambda c, s: (0, 0, 0))
    table_spec = pl.BlockSpec((PROMPTS, heads, width, width), lambda c, s: (0, 0, 0, 0))
    return pl.pallas_call(
        functools.partial(chunk_kernel, tokens // SPAN),
        grid_spec=pltpu.PrefetchScalarGridSpec(
            num_scalar_prefetch=1,
            grid=(tokens // rows,),
            in_specs=[token_spec, token_spec, token_spec, gate_spec, gate_spec],
            out_specs=[out_spec, out_spec, whole, whole, whole, table_spec],
            scratch_shapes=[
                pltpu.VMEM((rows * heads, width), F32),
                pltpu.VMEM((rows * heads, width), F32),
                pltpu.VMEM((rows * heads, width), F32),
                pltpu.VMEM((2 * SUBS, heads, width, 2 * width), F32),
                pltpu.VMEM((SUBS, heads, 2 * SPAN, 2 * width), F32),
                pltpu.VMEM((SUBS, heads, width, 2 * SPAN), BF16),
                pltpu.VMEM((heads, width, width), BF16),
                pltpu.VMEM((heads, width, width), BF16),
            ],
        ),
        out_shape=[
            jax.ShapeDtypeStruct((heads, tokens, width), F32),
            jax.ShapeDtypeStruct((heads, tokens, width), BF16),
            jax.ShapeDtypeStruct((heads, width, width), F32),
            jax.ShapeDtypeStruct((heads, width, width), BF16),
            jax.ShapeDtypeStruct((heads, width, width), BF16),
            jax.ShapeDtypeStruct((PROMPTS, heads, width, width), BF16),
        ],
        compiler_params=pltpu.CompilerParams(vmem_limit_bytes=VMEM_BYTES),
        cost_estimate=pl.CostEstimate(flops=6 * 10**9, bytes_accessed=16 * MIB, transcendentals=0),
        name="chunks",
    )(lengths, query, key, value, beta, gate)


def per_slot(ref, t, slots, heads, width):
    values = ref[t].astype(F32)
    return jnp.stack([jnp.broadcast_to(values[:, i : i + 1], (heads, width)) for i in range(slots)])


def request_kernel(probing, q_ref, k_ref, v_ref, beta_ref, gate_ref, out_ref, *scratch):
    slots, steps, heads, width = q_ref.shape
    keys = [unit(k_ref[:, t].astype(F32)) for t in range(steps)]
    queries = [unit(q_ref[:, t].astype(F32)) for t in range(steps)]
    gates, sources = [], []
    for t in range(steps):
        gate = per_slot(gate_ref, t, slots, heads, width)
        gates.append(gate if t == 0 else gates[-1] + gate)
    for t in range(steps):
        beta = per_slot(beta_ref, t, slots, heads, width)
        source = jnp.exp(gates[t]) * keys[t] if probing else v_ref[:, t].astype(F32)
        for s in range(t):
            factor = jnp.exp(gates[t] - gates[s]) * jnp.sum(keys[s] * keys[t], axis=-1, keepdims=True)
            source = source - factor * sources[s]
        sources.append(beta * source)
        result = jnp.exp(gates[t]) * queries[t] if probing else jnp.zeros_like(source)
        for s in range(t + 1):
            factor = jnp.sum(keys[s] * queries[t], axis=-1, keepdims=True)
            factor = factor if s == t else factor * jnp.exp(gates[t] - gates[s])
            result = result - factor * sources[s] if probing else result + factor * sources[s]
        if probing:
            scratch[0][pl.ds(t * slots * heads, slots * heads), :] = result.reshape(slots * heads, width)
        else:
            out_ref[t] = result
    if probing:
        for h in range(heads):
            out_ref[h] = scratch[0][pl.ds(h, steps * slots, stride=heads), :].astype(BF16)


def probe_kernel(q_ref, k_ref, beta_ref, gate_ref, out_ref, rows_ref):
    request_kernel(True, q_ref, k_ref, None, beta_ref, gate_ref, out_ref, rows_ref)


def request_probes(query, key, beta, gate):
    slots, steps, heads, width = query.shape
    return pl.pallas_call(
        probe_kernel,
        out_shape=jax.ShapeDtypeStruct((heads, steps * slots, width), BF16),
        scratch_shapes=[pltpu.VMEM((steps * slots * heads, width), F32)],
        compiler_params=pltpu.CompilerParams(vmem_limit_bytes=VMEM_BYTES),
        name="probes",
    )(query, key, beta, gate)


def request_locals(query, key, value, beta, gate):
    slots, steps, heads, width = query.shape
    return pl.pallas_call(
        functools.partial(request_kernel, False),
        out_shape=jax.ShapeDtypeStruct((steps, slots, heads, width), F32),
        compiler_params=pltpu.CompilerParams(vmem_limit_bytes=SMALL_BYTES),
        name="locals",
    )(query, key, value, beta, gate)


def reversed_bits(value, count):
    bits, turned = count.bit_length() - 1, 0
    for i in range(bits):
        turned |= ((value >> i) & 1) << (bits - 1 - i)
    return turned


def reversed_bits(value, count):
    bits, turned = count.bit_length() - 1, 0
    for i in range(bits):
        turned |= ((value >> i) & 1) << (bits - 1 - i)
    return turned


def spread_sources(source_ref, out_ref):
    _, peers, rows, _ = source_ref.shape
    me, mine = lax.axis_index("dec"), lax.axis_index("pre")
    for p in range(2):
        for x in range(peers):
            first = (p * peers + x) * rows
            peer = jnp.bitwise_xor(me, reversed_bits(x, peers))
            out_ref[first : first + rows, :] = jnp.broadcast_to(
                source_ref[lax.rem(mine + p, 2), peer], (rows, out_ref.shape[1])
            )


def stored_kernel(spans, lengths, table_ref, own_ref, other_ref, source_ref, keep_ref, send_ref, source_rows, total):
    peers, _, rows, width = own_ref.shape
    mine = lax.axis_index("pre")
    ends = prompt_ends(lengths)
    base = lax.axis_index("dec") * spans
    size = peers * rows

    @pl.when(pl.program_id(0) == 0)
    def _():
        spread_sources(source_ref, source_rows)

    total[...] = jnp.zeros_like(total)
    for j in range(PROMPTS):

        @pl.when(jnp.logical_and(ends[j] >= base, ends[j] < base + spans))
        def _(j=j):
            for first, ref in ((0, own_ref), (size, other_ref)):
                rows_here = slice(first, first + size)
                total[rows_here] = jnp.where(
                    source_rows[rows_here] == mine * PROMPTS + j,
                    dot(ref[:, 0].reshape(size, width), table_ref[j, 0]),
                    total[rows_here],
                )

    keep_ref[:, 0] = total[:size].astype(BF16).reshape(peers, rows, width)
    send_ref[:, 0] = total[size:].astype(BF16).reshape(peers, rows, width)


def stored_answers(lengths, spans, table, own, other, sources):
    peers, heads, rows, width = own.shape
    table_spec = pl.BlockSpec((PROMPTS, 1, width, width), lambda h, s: (0, h, 0, 0))
    rows_spec = pl.BlockSpec((peers, 1, rows, width), lambda h, s: (0, h, 0, 0))
    source_spec = pl.BlockSpec((2, peers, rows, 1), lambda h, s: (0, 0, 0, 0))
    out = jax.ShapeDtypeStruct(own.shape, BF16)
    return pl.pallas_call(
        functools.partial(stored_kernel, spans),
        grid_spec=pltpu.PrefetchScalarGridSpec(
            num_scalar_prefetch=1,
            grid=(heads,),
            in_specs=[table_spec, rows_spec, rows_spec, source_spec],
            out_specs=[rows_spec, rows_spec],
            scratch_shapes=[
                pltpu.VMEM((2 * peers * rows, width), jnp.int32),
                pltpu.VMEM((2 * peers * rows, width), F32),
            ],
        ),
        out_shape=[out, out],
        compiler_params=pltpu.CompilerParams(vmem_limit_bytes=16 * MIB),
        cost_estimate=pl.CostEstimate(flops=10**9, bytes_accessed=16 * MIB, transcendentals=0),
        name="stored",
    )(lengths, table, own, other, sources)


def carried_kernel(
    spans,
    lengths,
    state_ref,
    first_ref,
    second_ref,
    first_got_ref,
    second_got_ref,
    own_ref,
    other_ref,
    own_part_ref,
    other_part_ref,
    source_ref,
    sent_ref,
    keep_ref,
    send_ref,
    source_rows,
):
    peers, heads, rows, width = own_ref.shape
    mine = lax.axis_index("pre")
    ends = prompt_ends(lengths)
    base = lax.axis_index("dec") * spans
    size = peers * rows
    through = jnp.where(first_end_in(ends, base, spans) < spans, 0.0, 1.0)
    next_end = base + spans + first_end_in(ends, base + spans, spans)
    next_prompt = jnp.int32(-1)
    for j in range(PROMPTS):
        next_prompt = jnp.where(ends[j] == next_end, mine * PROMPTS + j, next_prompt)
    spread_sources(source_ref, source_rows)
    odd = jnp.full((width, width), lax.rem(lax.axis_index("dec"), 2)) == 1
    leaving, carried = [], []
    for h in range(heads):
        own_map = jnp.where(odd, first_ref[h], second_ref[h])
        arrived = jnp.where(odd, first_got_ref[h], second_got_ref[h])
        leaving.append((state_ref[h] + through * dot(own_map, arrived)).astype(BF16))
    for h in range(heads):
        next_map = jnp.where(odd, second_got_ref[h], first_got_ref[h])
        carried.append(dot(next_map, leaving[h]).astype(BF16))
    for h in range(heads):
        sent_ref[h] = leaving[h]
        for first, ref, part, out in (
            (0, own_ref, own_part_ref, keep_ref),
            (size, other_ref, other_part_ref, send_ref),
        ):
            out[:, h] = (
                jnp.where(
                    source_rows[first : first + size] == next_prompt,
                    dot(ref[:, h].reshape(size, width), carried[h]),
                    part[:, h].reshape(size, width).astype(F32),
                )
                .astype(BF16)
                .reshape(peers, rows, width)
            )


def carried_answers(lengths, spans, state, first, second, own, other, own_part, other_part, sources):
    peers, heads, rows, width = own.shape
    out = jax.ShapeDtypeStruct(own.shape, BF16)
    return pl.pallas_call(
        functools.partial(carried_kernel, spans),
        grid_spec=pltpu.PrefetchScalarGridSpec(
            num_scalar_prefetch=1,
            grid=(1,),
            in_specs=[pl.BlockSpec(memory_space=pltpu.VMEM)] * 10,
            out_specs=[pl.BlockSpec(memory_space=pltpu.VMEM)] * 3,
            scratch_shapes=[pltpu.VMEM((2 * peers * rows, width), jnp.int32)],
        ),
        out_shape=[jax.ShapeDtypeStruct((heads, width, width), BF16), out, out],
        compiler_params=pltpu.CompilerParams(vmem_limit_bytes=CARRIED_MIB * MIB),
        name="carried",
    )(lengths, state, first[0], second[0], first[1], second[1], own, other, own_part, other_part, sources)


def emit_kernel(local_ref, probe_ref, entry_ref, out_ref, rows_ref):
    heads, rows, width = local_ref.shape
    for h in range(heads):
        rows_ref[pl.ds(h, rows, stride=heads), :] = local_ref[h] + dot(probe_ref[h], entry_ref[h])
    out_ref[...] = rows_ref[...].reshape(rows, heads, width).astype(BF16)


def emit(local, probe, entry):
    heads, tokens, width = local.shape
    rows = EMIT_ROWS
    spec = pl.BlockSpec((heads, rows, width), lambda c: (0, c, 0))
    return pl.pallas_call(
        emit_kernel,
        grid=(tokens // rows,),
        in_specs=[spec, spec, pl.BlockSpec((heads, width, width), lambda c: (0, 0, 0))],
        out_specs=pl.BlockSpec((rows, heads, width), lambda c: (c, 0, 0)),
        out_shape=jax.ShapeDtypeStruct((tokens, heads, width), BF16),
        scratch_shapes=[pltpu.VMEM((rows * heads, width), F32)],
        compiler_params=pltpu.CompilerParams(vmem_limit_bytes=EMIT_BYTES),
        cost_estimate=pl.CostEstimate(flops=10**9, bytes_accessed=8 * MIB, transcendentals=0),
        name="emit",
    )(local, probe, entry)


def finish_kernel(live, mine_ref, near_ref, far_ref, local_ref, out_ref, rows_ref):
    slots, steps, heads, width = out_ref.shape
    for h in range(heads):
        rows_ref[pl.ds(h, steps * slots, stride=heads), :] = (
            mine_ref[0, h].astype(F32) + near_ref[0, h].astype(F32)
        ) + far_ref[0, h].astype(F32)
    on = iota2((slots, heads, width), 0) < live[0]
    for t in range(steps):
        part = rows_ref[pl.ds(t * slots * heads, slots * heads), :].reshape(slots, heads, width)
        out_ref[:, t] = jnp.where(on, part + local_ref[t], 0.0).astype(BF16)


def finish(live, mine, near, far, local):
    steps, slots, heads, width = local.shape
    return pl.pallas_call(
        finish_kernel,
        grid_spec=pltpu.PrefetchScalarGridSpec(
            num_scalar_prefetch=1,
            grid=(1,),
            in_specs=[
                pl.BlockSpec((1,) + mine.shape[1:], lambda i, s: (0, 0, 0, 0)),
                pl.BlockSpec((1,) + near.shape[1:], lambda i, s: (0, 0, 0, 0)),
                pl.BlockSpec((1,) + far.shape[1:], lambda i, s: (0, 0, 0, 0)),
                pl.BlockSpec(local.shape, lambda i, s: (0, 0, 0, 0)),
            ],
            out_specs=pl.BlockSpec((slots, steps, heads, width), lambda i, s: (0, 0, 0, 0)),
            scratch_shapes=[pltpu.VMEM((steps * slots * heads, width), F32)],
        ),
        out_shape=jax.ShapeDtypeStruct((slots, steps, heads, width), BF16),
        compiler_params=pltpu.CompilerParams(vmem_limit_bytes=SMALL_BYTES),
        name="finish",
    )(live, mine, near, far, local)


def shifted(array, by):
    peers = lax.axis_size("dec")
    return lax.ppermute(array, "dec", [(i, i + by) for i in range(peers) if 0 <= i + by < peers])


def added(left, right):
    return (left.astype(F32) + right.astype(F32)).astype(BF16)


def local(
    prompt_query,
    prompt_key,
    prompt_value,
    prompt_beta,
    prompt_gate,
    prompt_lengths,
    request_source_prompt,
    live_counts,
    decode_query,
    decode_key,
    decode_value,
    decode_beta,
    decode_gate,
):
    peers = lax.axis_size("dec")
    tokens = prompt_query.shape[1]
    spans = tokens // SPAN
    steps = decode_query.shape[1]
    longest = peers * spans // 2
    hops = max(1, (longest - 2) // spans + 1)
    step_beta = jnp.transpose(decode_beta, (1, 2, 0))
    step_gate = jnp.transpose(decode_gate, (1, 2, 0))
    probes = request_probes(decode_query, decode_key, step_beta, step_gate)
    own_probes = [probes]
    for x in range(1, peers):
        pairs = [(i, i ^ reversed_bits(x, peers)) for i in range(peers)]
        own_probes.append(lax.ppermute(probes, "dec", pairs))
    probes, prompt_key = lax.optimization_barrier((probes, prompt_key))
    sources = request_source_prompt.reshape(2, peers, 1, -1)
    slots = sources.shape[3]
    sources = jnp.broadcast_to(sources, (2, peers, steps, slots)).reshape(2, peers, steps * slots, 1)

    chunk_local, chunk_probe, state, first, second, table = prefill(
        prompt_lengths, prompt_query[0], prompt_key[0], prompt_value[0], prompt_beta[0], prompt_gate[0]
    )
    own_probes, first, second, decode_value = lax.optimization_barrier(
        (own_probes, first, second, decode_value)
    )
    decode_local = request_locals(decode_query, decode_key, decode_value, step_beta, step_gate)
    pairs = [(i, i ^ 1) for i in range(peers)]
    first_got = lax.ppermute(first, "dec", pairs)
    pairs = [(i, (i + 1 ^ 1) - 1) for i in range(1, peers - 1)]
    second_got = lax.ppermute(second, "dec", pairs)
    if hops > 2:
        odd = lax.axis_index("dec") % 2 == 1
        ends = jnp.cumsum(prompt_lengths[0]) - 1
        closed = jnp.any(ends // spans == lax.axis_index("dec"))
        own_map = jnp.where(odd, first, second)
        through = jnp.where(closed, 0.0, own_map.astype(F32)).astype(BF16)

        def turn(_, arriving):
            leaving = state + jnp.einsum("hij,hjk->hik", through, arriving, preferred_element_type=F32)
            return shifted(leaving.astype(BF16), 1)

        arrived = lax.fori_loop(0, hops - 2, turn, jnp.where(odd, first_got, second_got))
        first_got, second_got = (
            jnp.where(odd, arrived, first_got),
            jnp.where(odd, second_got, arrived),
        )
    own_probes = jnp.stack(own_probes)
    other_probes = lax.ppermute(own_probes, "pre", [(0, 1), (1, 0)])
    own_part, other_part = stored_answers(prompt_lengths, spans, table, own_probes, other_probes, sources)
    leaving, keep, send = carried_answers(
        prompt_lengths,
        spans,
        state,
        (first, first_got),
        (second, second_got),
        own_probes,
        other_probes,
        own_part,
        other_part,
        sources,
    )
    theirs = lax.ppermute(send, "pre", [(0, 1), (1, 0)])
    entry = shifted(leaving, 1)
    block = added(keep, theirs)
    theirs = jnp.zeros_like(block)
    bit, part = 1, peers // 2
    while part:
        pairs = [(i, i ^ bit) for i in range(peers)]
        if bit == 1:
            outgoing = block[part:]
        else:
            outgoing = added(block[part : 2 * part], theirs[part : 2 * part])
        if bit > 1 and part > 1:
            block = added(block[:part], theirs[:part])
        before, theirs = theirs, lax.ppermute(outgoing, "dec", pairs)
        bit, part = 2 * bit, part // 2
    step_result = finish(live_counts, block, before, theirs, decode_local)
    prompt_result = emit(chunk_local, chunk_probe, entry)[None]
    return (prompt_result, step_result)


def solution(mesh):
    in_specs = (
        P("pre", "dec", "head", None),
        P("pre", "dec", "head", None),
        P("pre", "dec", "head", None),
        P("pre", "head", "dec"),
        P("pre", "head", "dec"),
        P("pre", None),
        P(),
        P(("pre", "dec")),
        P(("pre", "dec"), None, "head", None),
        P(("pre", "dec"), None, "head", None),
        P(("pre", "dec"), None, "head", None),
        P(("pre", "dec"), None, "head"),
        P(("pre", "dec"), None, "head"),
    )
    out_specs = (P("pre", "dec", "head", None), P(("pre", "dec"), None, "head", None))
    return jax.shard_map(local, mesh=mesh, in_specs=in_specs, out_specs=out_specs, check_vma=False)
```

```python
import functools

import jax
import jax.numpy as jnp
from jax import lax
from jax.experimental import pallas as pl
from jax.experimental.pallas import tpu as pltpu
from jax.sharding import PartitionSpec as P

SPAN = 64
PROMPTS = 4
F32 = jnp.float32
BF16 = jnp.bfloat16
MIB = 1024 * 1024
VMEM_BYTES = 60 * MIB
SMALL_BYTES = 16 * MIB
EMIT_BYTES = 20 * MIB
CARRIED_MIB = 48
EMIT_ROWS = 256
BASE = 64
SUBS = 2


def dot(left, right):
    return jnp.dot(left, right, preferred_element_type=F32)


def dot_split(left, right):
    width = right.shape[1] // 2
    high = right.astype(BF16)
    low = (right[:, :width] - high[:, :width].astype(F32)).astype(BF16)
    both = dot(left, high)
    return jnp.concatenate([both[:, :width] + dot(left, low), both[:, width:]], axis=1)


def dot_last(left, right):
    return lax.dot_general(left, right, (((1,), (1,)), ((), ())), preferred_element_type=F32)


def scale_of(rows):
    return lax.rsqrt(jnp.sum(rows * rows, axis=-1, keepdims=True) + 1e-06)


def unit(rows):
    return rows * scale_of(rows)


def iota2(shape, dim):
    return lax.broadcasted_iota(jnp.int32, shape, dim)


def any_equal(marks, value):
    found = marks[0] == value
    for mark in marks[1:]:
        found = jnp.logical_or(found, mark == value)
    return found


def prompt_ends(lengths):
    ends = [lengths[0, 0] - 1]
    for j in range(1, PROMPTS):
        ends.append(ends[-1] + lengths[0, j])
    return ends


def first_end_in(ends, first, count):
    found = jnp.int32(count)
    for end in reversed(ends):
        inside = jnp.logical_and(end >= first, end < first + count)
        found = jnp.where(inside, end - first, found)
    return found


def tiled(part, size):
    return jnp.concatenate([part] * (size // part.shape[0]), axis=0)


def inverse_of(lower, masks, group):
    size = lower[0].shape[0]
    heads = range(group)
    zero = jnp.zeros((size, size), BF16)

    def packed(h, width):
        parts = [
            jnp.where(masks["lanes", width, b], lower[h][b * width : (b + 1) * width], 0.0)
            for b in range(size // width)
        ]
        return functools.reduce(lambda x, y: x + y, parts)

    def spread(part, mask):
        return jnp.where(mask, tiled(part, size), zero)

    small = [packed(h, BASE) for h in heads]
    inverse = [masks["eye"] - small[h] for h in heads]
    part = [small[h].astype(BF16) for h in heads]
    full = [spread(part[h], masks["same", BASE]) for h in heads]
    part = [dot(part[h], full[h]).astype(BF16) for h in heads]
    power = 2
    while power < BASE:
        full = [spread(part[h], masks["same", BASE]) for h in heads]
        if 2 * power < BASE:
            both = [
                dot(jnp.concatenate([part[h], inverse[h].astype(BF16)], axis=0), full[h])
                for h in heads
            ]
            part = [both[h][:BASE].astype(BF16) for h in heads]
            inverse = [inverse[h] + both[h][BASE:] for h in heads]
        else:
            inverse = [inverse[h] + dot(inverse[h].astype(BF16), full[h]) for h in heads]
        power *= 2
    inverse = [inverse[h].astype(BF16) for h in heads]
    full = [spread(inverse[h], masks["same", BASE]) for h in heads]
    width = BASE
    while width < size:
        below = []
        for h in heads:
            parts = [
                jnp.where(
                    masks["lanes", width, 2 * b],
                    lower[h][(2 * b + 1) * width : (2 * b + 2) * width],
                    0.0,
                )
                for b in range(size // (2 * width))
            ]
            below.append(functools.reduce(lambda x, y: x + y, parts).astype(BF16))
        turned = [dot(below[h], full[h]).astype(BF16) for h in heads]
        wide = [spread(turned[h], masks["off", width]) for h in heads]
        corner = [-dot(inverse[h], wide[h]) for h in heads]
        even = masks["even", width]
        corner = [corner[h].astype(BF16) for h in heads]
        inverse = [
            jnp.concatenate(
                [
                    jnp.where(even, inverse[h], jnp.zeros_like(inverse[h])),
                    jnp.where(even, corner[h], inverse[h]),
                ],
                axis=0,
            )
            for h in heads
        ]
        width *= 2
        if width < size:
            full = [spread(inverse[h], masks["same", width]) for h in heads]
    return inverse


def masks_of(size):
    row = iota2((size, size), 0)
    col = iota2((size, size), 1)
    masks = {"eye": (iota2((BASE, size), 0) == iota2((BASE, size), 1) % BASE).astype(F32)}
    width = BASE
    while width < size:
        masks["same", width] = (row // width) == (col // width)
        masks["off", width] = jnp.logical_and(
            (row // (2 * width)) == (col // (2 * width)), (row // width) != (col // width)
        )
        lanes = iota2((width, size), 1) // width
        for b in range(size // width):
            masks["lanes", width, b] = lanes == b
        masks["even", width] = lanes % 2 == 0
        width *= 2
    return masks


def chunk_kernel(
    spans,
    lengths,
    q_ref,
    k_ref,
    v_ref,
    beta_ref,
    gate_ref,
    local_ref,
    probe_ref,
    state_ref,
    first_ref,
    second_ref,
    table_ref,
    qf,
    kf,
    vf,
    walk,
    fresh,
    turned_keys,
    half_map,
    own_map,
):
    turn = pl.program_id(0)
    block_rows, heads, width = k_ref.shape
    rows = 2 * SPAN
    subs = block_rows // rows
    half = rows // 2
    places = 2 * subs

    @pl.when(turn == 0)
    def _():
        eye = (iota2((width, width), 0) == iota2((width, width), 1)).astype(F32)
        for h in range(heads):
            walk[0, h, :, :width] = jnp.zeros((width, width), F32)
            walk[0, h, :, width:] = eye
        table_ref[...] = jnp.zeros_like(table_ref)

    base = lax.axis_index("dec") * spans
    ends = [end - base for end in prompt_ends(lengths)]
    starts = [-base] + [end + 1 for end in ends[:-1]]
    map_block = jnp.minimum(first_end_in(ends, 0, spans), spans - 1)
    first_place = lax.rem(turn, 2) * subs
    first_block = 2 * subs * turn
    keeps = [
        1.0 - any_equal(starts, first_block + i).astype(F32)
        for i in range(2 * subs)
    ]

    qf[...] = q_ref[...].astype(F32).reshape(block_rows * heads, width)
    kf[...] = k_ref[...].astype(F32).reshape(block_rows * heads, width)
    vf[...] = v_ref[...].astype(F32).reshape(block_rows * heads, width)

    row = iota2((rows, rows), 0)
    col = iota2((rows, rows), 1)
    strict = row > col
    diagonal = row == col
    masks = masks_of(rows)
    lowers, row_opens, tail_opens, totals, total_cols, beta_cols = [], [], [], [], [], []
    for s in range(subs):
        keep1 = keeps[2 * s + 1]
        open_pair = jnp.logical_or(
            (row >= half) == (col >= half), jnp.full((rows, rows), keep1) > 0.5
        )
        lowers.append(jnp.logical_and(row >= col, open_pair))
        row_opens.append(jnp.where(iota2((rows, 1), 0) >= half, keep1, 1.0))
        tail_opens.append(jnp.where(iota2((rows, 1), 0) < half, keep1, 1.0))
        total = lax.dot_general(
            gate_ref[:, s * rows : (s + 1) * rows],
            (row <= col).astype(F32),
            (((1,), (0,)), ((), ())),
            precision=lax.Precision.HIGHEST,
            preferred_element_type=F32,
        )
        totals.append(total)
        total_cols.append(jnp.transpose(total))
        beta_cols.append(jnp.transpose(beta_ref[:, s * rows : (s + 1) * rows]))

    units = [(s, h) for s in range(subs) for h in range(heads)]
    idx = range(len(units))

    def rows_of(ref, s, h):
        return ref[pl.ds(s * rows * heads + h, rows, stride=heads), :]

    keys = [rows_of(kf, s, h) for s, h in units]
    queries = [rows_of(qf, s, h) for s, h in units]
    keys_half = [x.astype(BF16) for x in keys]
    queries_half = [x.astype(BF16) for x in queries]
    grams = [
        dot_last(jnp.concatenate([keys_half[i], queries_half[i]], axis=0), keys_half[i])
        for i in idx
    ]
    key_col = [scale_of(keys[i]) for i in idx]
    query_col = [scale_of(queries[i]) for i in idx]
    key_row = [
        lax.rsqrt(
            jnp.sum(jnp.where(diagonal, grams[i][:rows], 0.0), axis=0, keepdims=True) + 1e-06
        )
        for i in idx
    ]
    sums_col = [total_cols[s][:, h : h + 1] for s, h in units]
    sums_row = [totals[s][h : h + 1, :] for s, h in units]
    betas = [beta_cols[s][:, h : h + 1] for s, h in units]
    decays = [
        jnp.exp(jnp.where(lowers[units[i][0]], sums_col[i] - sums_row[i], -1e30)) * key_row[i]
        for i in idx
    ]
    strict_part = [
        jnp.where(strict, (betas[i] * key_col[i]) * (decays[i] * grams[i][:rows]), 0.0)
        for i in idx
    ]
    scores = [(query_col[i] * (decays[i] * grams[i][rows:])).astype(BF16) for i in idx]
    growth = [jnp.exp(sums_col[i]) * row_opens[units[i][0]] for i in idx]
    inverse = inverse_of(strict_part, masks, len(units))
    right = [
        jnp.concatenate(
            [
                (keys[i] * (betas[i] * growth[i] * key_col[i])).astype(BF16),
                (rows_of(vf, *units[i]) * betas[i]).astype(BF16),
            ],
            axis=1,
        )
        for i in idx
    ]
    wu = [dot(inverse[i], right[i]) for i in idx]
    turned = [jnp.transpose(keys_half[i]) for i in idx]
    tails = [
        jnp.exp(sums_row[i][:, rows - 1 :] - sums_col[i]) * (key_col[i] * tail_opens[units[i][0]])
        for i in idx
    ]
    grown = [(queries[i] * (growth[i] * query_col[i])).astype(BF16) for i in idx]
    entry = [walk[first_place, h] for h in range(heads)]
    for s in range(subs):
        mine = [s * heads + h for h in range(heads)]
        entry = [x * keeps[2 * s] for x in entry]
        entry_half = [x.astype(BF16) for x in entry]
        moved = [dot(wu[i][:, :width].astype(BF16), entry_half[i % heads]) for i in mine]
        new = [
            jnp.concatenate(
                [
                    wu[i][:, width:] - moved[i % heads][:, :width],
                    -moved[i % heads][:, width:],
                ],
                axis=1,
            )
            for i in mine
        ]
        for h in range(heads):
            fresh[s, h] = new[h]
        leaving = [
            entry[i % heads] * (jnp.exp(sums_row[i][:, rows - 1 :]) * keeps[2 * s + 1])
            + dot_split(turned[i], new[i % heads] * tails[i])
            for i in mine
        ]
        new = [x.astype(BF16) for x in new]
        outs = [
            dot(
                jnp.concatenate([grown[i], scores[i]], axis=1),
                jnp.concatenate([entry_half[i % heads], new[i % heads]], axis=0),
            )
            for i in mine
        ]
        place = lax.rem(first_place + s + 1, places)
        for h in range(heads):
            walk[place, h] = leaving[h]
            turned_keys[s, h] = turned[mine[h]]
            local_ref[h, s * rows : (s + 1) * rows] = outs[h][:, :width]
            probe_ref[h, s * rows : (s + 1) * rows] = outs[h][:, width:].astype(BF16)
        entry = leaving

    for s in range(subs):
        block0 = first_block + 2 * s
        now = lax.rem(first_place + s, places)
        later = lax.rem(first_place + s + 1, places)

        @pl.when(any_equal(ends, block0))
        def _(s=s, block0=block0, now=now):
            prompt = jnp.int32(0)
            for j in range(1, PROMPTS):
                prompt = jnp.where(ends[j] == block0, j, prompt)
            at_half = [totals[s][h : h + 1, half - 1 : half] for h in range(heads)]
            first_half = iota2((rows, 1), 0) < half
            weights = [
                jnp.exp(jnp.where(first_half, at_half[h] - total_cols[s][:, h : h + 1], -1e30))
                for h in range(heads)
            ]
            weights = [weights[h] * scale_of(rows_of(kf, s, h)) for h in range(heads)]
            steps = [dot_split(turned_keys[s, h], fresh[s, h] * weights[h]) for h in range(heads)]
            for h in range(heads):
                state = walk[now, h] * (keeps[2 * s] * jnp.exp(at_half[h])) + steps[h]
                table_ref[prompt, h] = state[:, :width].astype(BF16)
                half_map[h] = state[:, width:].astype(BF16)

            @pl.when(map_block == block0)
            def _():
                own_map[...] = half_map[...]

        for j in range(PROMPTS):

            @pl.when(ends[j] == block0 + 1)
            def _(j=j, later=later):
                table_ref[j] = walk[later, :, :, :width].astype(BF16)

        @pl.when(map_block == block0 + 1)
        def _(later=later):
            own_map[...] = walk[later, :, :, width:].astype(BF16)

    @pl.when(turn == pl.num_programs(0) - 1)
    def _():
        last = walk[lax.rem(first_place + subs, places), :, :, :width]
        state_ref[...] = last
        odd = jnp.full(last.shape, lax.rem(lax.axis_index("dec"), 2)) == 1
        first_ref[...] = jnp.where(odd, own_map[...], last.astype(BF16))
        second_ref[...] = jnp.where(odd, last.astype(BF16), own_map[...])


def prefill(lengths, query, key, value, beta, gate):
    tokens, heads, width = key.shape
    rows = 2 * SPAN * SUBS
    token_spec = pl.BlockSpec((rows, heads, width), lambda c, s: (c, 0, 0))
    gate_spec = pl.BlockSpec((heads, rows), lambda c, s: (0, c))
    out_spec = pl.BlockSpec((heads, rows, width), lambda c, s: (0, c, 0))
    whole = pl.BlockSpec((heads, width, width), lambda c, s: (0, 0, 0))
    table_spec = pl.BlockSpec((PROMPTS, heads, width, width), lambda c, s: (0, 0, 0, 0))
    return pl.pallas_call(
        functools.partial(chunk_kernel, tokens // SPAN),
        grid_spec=pltpu.PrefetchScalarGridSpec(
            num_scalar_prefetch=1,
            grid=(tokens // rows,),
            in_specs=[token_spec, token_spec, token_spec, gate_spec, gate_spec],
            out_specs=[out_spec, out_spec, whole, whole, whole, table_spec],
            scratch_shapes=[
                pltpu.VMEM((rows * heads, width), F32),
                pltpu.VMEM((rows * heads, width), F32),
                pltpu.VMEM((rows * heads, width), F32),
                pltpu.VMEM((2 * SUBS, heads, width, 2 * width), F32),
                pltpu.VMEM((SUBS, heads, 2 * SPAN, 2 * width), F32),
                pltpu.VMEM((SUBS, heads, width, 2 * SPAN), BF16),
                pltpu.VMEM((heads, width, width), BF16),
                pltpu.VMEM((heads, width, width), BF16),
            ],
        ),
        out_shape=[
            jax.ShapeDtypeStruct((heads, tokens, width), F32),
            jax.ShapeDtypeStruct((heads, tokens, width), BF16),
            jax.ShapeDtypeStruct((heads, width, width), F32),
            jax.ShapeDtypeStruct((heads, width, width), BF16),
            jax.ShapeDtypeStruct((heads, width, width), BF16),
            jax.ShapeDtypeStruct((PROMPTS, heads, width, width), BF16),
        ],
        compiler_params=pltpu.CompilerParams(vmem_limit_bytes=VMEM_BYTES),
        cost_estimate=pl.CostEstimate(flops=6 * 10**9, bytes_accessed=16 * MIB, transcendentals=0),
        name="chunks",
    )(lengths, query, key, value, beta, gate)


def request_kernel(q_ref, k_ref, v_ref, beta_ref, gate_ref, probe_ref, local_ref, rows_ref):
    slots, steps, heads, width = q_ref.shape

    def per_slot(ref, t):
        values = ref[t].astype(F32)
        return jnp.stack(
            [jnp.broadcast_to(values[:, i : i + 1], (heads, width)) for i in range(slots)]
        )

    keys = [unit(k_ref[:, t].astype(F32)) for t in range(steps)]
    queries = [unit(q_ref[:, t].astype(F32)) for t in range(steps)]
    gates = []
    for t in range(steps):
        gate = per_slot(gate_ref, t)
        gates.append(gate if t == 0 else gates[-1] + gate)
    weights, updates = [], []
    for t in range(steps):
        beta = per_slot(beta_ref, t)
        reach = jnp.exp(gates[t]) * keys[t]
        value = v_ref[:, t].astype(F32)
        for s in range(t):
            factor = jnp.exp(gates[t] - gates[s]) * jnp.sum(keys[s] * keys[t], axis=-1, keepdims=True)
            reach = reach - factor * weights[s]
            value = value - factor * updates[s]
        weights.append(beta * reach)
        updates.append(beta * value)
        probe = jnp.exp(gates[t]) * queries[t]
        emitted = jnp.zeros_like(value)
        for s in range(t + 1):
            factor = jnp.sum(keys[s] * queries[t], axis=-1, keepdims=True)
            factor = factor if s == t else factor * jnp.exp(gates[t] - gates[s])
            probe = probe - factor * weights[s]
            emitted = emitted + factor * updates[s]
        rows_ref[pl.ds(t * slots * heads, slots * heads), :] = probe.reshape(slots * heads, width)
        local_ref[t] = emitted
    for h in range(heads):
        probe_ref[h] = rows_ref[pl.ds(h, steps * slots, stride=heads), :].astype(BF16)


def requests(query, key, value, beta, gate):
    slots, steps, heads, width = query.shape
    beta, gate = jnp.transpose(beta, (1, 2, 0)), jnp.transpose(gate, (1, 2, 0))
    return pl.pallas_call(
        request_kernel,
        out_shape=[
            jax.ShapeDtypeStruct((heads, steps * slots, width), BF16),
            jax.ShapeDtypeStruct((steps, slots, heads, width), F32),
        ],
        scratch_shapes=[pltpu.VMEM((steps * slots * heads, width), F32)],
        compiler_params=pltpu.CompilerParams(vmem_limit_bytes=VMEM_BYTES),
        name="requests",
    )(query, key, value, beta, gate)


def reversed_bits(value, count):
    bits, turned = count.bit_length() - 1, 0
    for i in range(bits):
        turned |= ((value >> i) & 1) << (bits - 1 - i)
    return turned


def reversed_bits(value, count):
    bits, turned = count.bit_length() - 1, 0
    for i in range(bits):
        turned |= ((value >> i) & 1) << (bits - 1 - i)
    return turned


def spread_sources(source_ref, out_ref):
    _, peers, rows, _ = source_ref.shape
    me, mine = lax.axis_index("dec"), lax.axis_index("pre")
    for p in range(2):
        for x in range(peers):
            first = (p * peers + x) * rows
            peer = jnp.bitwise_xor(me, reversed_bits(x, peers))
            out_ref[first : first + rows, :] = jnp.broadcast_to(
                source_ref[lax.rem(mine + p, 2), peer], (rows, out_ref.shape[1])
            )


def stored_kernel(spans, lengths, table_ref, own_ref, other_ref, source_ref, keep_ref, send_ref, source_rows, total):
    peers, _, rows, width = own_ref.shape
    mine = lax.axis_index("pre")
    ends = prompt_ends(lengths)
    base = lax.axis_index("dec") * spans
    size = peers * rows

    @pl.when(pl.program_id(0) == 0)
    def _():
        spread_sources(source_ref, source_rows)

    total[...] = jnp.zeros_like(total)
    for j in range(PROMPTS):

        @pl.when(jnp.logical_and(ends[j] >= base, ends[j] < base + spans))
        def _(j=j):
            for first, ref in ((0, own_ref), (size, other_ref)):
                rows_here = slice(first, first + size)
                total[rows_here] = jnp.where(
                    source_rows[rows_here] == mine * PROMPTS + j,
                    dot(ref[:, 0].reshape(size, width), table_ref[j, 0]),
                    total[rows_here],
                )

    keep_ref[:, 0] = total[:size].astype(BF16).reshape(peers, rows, width)
    send_ref[:, 0] = total[size:].astype(BF16).reshape(peers, rows, width)


def stored_answers(lengths, spans, table, own, other, sources):
    peers, heads, rows, width = own.shape
    table_spec = pl.BlockSpec((PROMPTS, 1, width, width), lambda h, s: (0, h, 0, 0))
    rows_spec = pl.BlockSpec((peers, 1, rows, width), lambda h, s: (0, h, 0, 0))
    source_spec = pl.BlockSpec((2, peers, rows, 1), lambda h, s: (0, 0, 0, 0))
    out = jax.ShapeDtypeStruct(own.shape, BF16)
    return pl.pallas_call(
        functools.partial(stored_kernel, spans),
        grid_spec=pltpu.PrefetchScalarGridSpec(
            num_scalar_prefetch=1,
            grid=(heads,),
            in_specs=[table_spec, rows_spec, rows_spec, source_spec],
            out_specs=[rows_spec, rows_spec],
            scratch_shapes=[
                pltpu.VMEM((2 * peers * rows, width), jnp.int32),
                pltpu.VMEM((2 * peers * rows, width), F32),
            ],
        ),
        out_shape=[out, out],
        compiler_params=pltpu.CompilerParams(vmem_limit_bytes=16 * MIB),
        cost_estimate=pl.CostEstimate(flops=10**9, bytes_accessed=16 * MIB, transcendentals=0),
        name="stored",
    )(lengths, table, own, other, sources)


def carried_kernel(
    spans,
    lengths,
    state_ref,
    first_ref,
    second_ref,
    first_got_ref,
    second_got_ref,
    own_ref,
    other_ref,
    own_part_ref,
    other_part_ref,
    source_ref,
    sent_ref,
    keep_ref,
    send_ref,
    source_rows,
):
    peers, heads, rows, width = own_ref.shape
    mine = lax.axis_index("pre")
    ends = prompt_ends(lengths)
    base = lax.axis_index("dec") * spans
    size = peers * rows
    through = jnp.where(first_end_in(ends, base, spans) < spans, 0.0, 1.0)
    next_end = base + spans + first_end_in(ends, base + spans, spans)
    next_prompt = jnp.int32(-1)
    for j in range(PROMPTS):
        next_prompt = jnp.where(ends[j] == next_end, mine * PROMPTS + j, next_prompt)
    spread_sources(source_ref, source_rows)
    odd = jnp.full((width, width), lax.rem(lax.axis_index("dec"), 2)) == 1
    leaving, carried = [], []
    for h in range(heads):
        own_map = jnp.where(odd, first_ref[h], second_ref[h])
        arrived = jnp.where(odd, first_got_ref[h], second_got_ref[h])
        leaving.append((state_ref[h] + through * dot(own_map, arrived)).astype(BF16))
    for h in range(heads):
        next_map = jnp.where(odd, second_got_ref[h], first_got_ref[h])
        carried.append(dot(next_map, leaving[h]).astype(BF16))
    for h in range(heads):
        sent_ref[h] = leaving[h]
        for first, ref, part, out in (
            (0, own_ref, own_part_ref, keep_ref),
            (size, other_ref, other_part_ref, send_ref),
        ):
            out[:, h] = (
                jnp.where(
                    source_rows[first : first + size] == next_prompt,
                    dot(ref[:, h].reshape(size, width), carried[h]),
                    part[:, h].reshape(size, width).astype(F32),
                )
                .astype(BF16)
                .reshape(peers, rows, width)
            )


def carried_answers(lengths, spans, state, first, second, own, other, own_part, other_part, sources):
    peers, heads, rows, width = own.shape
    out = jax.ShapeDtypeStruct(own.shape, BF16)
    return pl.pallas_call(
        functools.partial(carried_kernel, spans),
        grid_spec=pltpu.PrefetchScalarGridSpec(
            num_scalar_prefetch=1,
            grid=(1,),
            in_specs=[pl.BlockSpec(memory_space=pltpu.VMEM)] * 10,
            out_specs=[pl.BlockSpec(memory_space=pltpu.VMEM)] * 3,
            scratch_shapes=[pltpu.VMEM((2 * peers * rows, width), jnp.int32)],
        ),
        out_shape=[jax.ShapeDtypeStruct((heads, width, width), BF16), out, out],
        compiler_params=pltpu.CompilerParams(vmem_limit_bytes=CARRIED_MIB * MIB),
        name="carried",
    )(lengths, state, first[0], second[0], first[1], second[1], own, other, own_part, other_part, sources)


def emit_kernel(local_ref, probe_ref, entry_ref, out_ref, rows_ref):
    heads, rows, width = local_ref.shape
    for h in range(heads):
        rows_ref[pl.ds(h, rows, stride=heads), :] = local_ref[h] + dot(probe_ref[h], entry_ref[h])
    out_ref[...] = rows_ref[...].reshape(rows, heads, width).astype(BF16)


def emit(local, probe, entry):
    heads, tokens, width = local.shape
    rows = EMIT_ROWS
    spec = pl.BlockSpec((heads, rows, width), lambda c: (0, c, 0))
    return pl.pallas_call(
        emit_kernel,
        grid=(tokens // rows,),
        in_specs=[spec, spec, pl.BlockSpec((heads, width, width), lambda c: (0, 0, 0))],
        out_specs=pl.BlockSpec((rows, heads, width), lambda c: (c, 0, 0)),
        out_shape=jax.ShapeDtypeStruct((tokens, heads, width), BF16),
        scratch_shapes=[pltpu.VMEM((rows * heads, width), F32)],
        compiler_params=pltpu.CompilerParams(vmem_limit_bytes=EMIT_BYTES),
        cost_estimate=pl.CostEstimate(flops=10**9, bytes_accessed=8 * MIB, transcendentals=0),
        name="emit",
    )(local, probe, entry)


def finish_kernel(live, mine_ref, near_ref, far_ref, local_ref, out_ref, rows_ref):
    slots, steps, heads, width = out_ref.shape
    for h in range(heads):
        rows_ref[pl.ds(h, steps * slots, stride=heads), :] = (
            mine_ref[0, h].astype(F32) + near_ref[0, h].astype(F32)
        ) + far_ref[0, h].astype(F32)
    on = iota2((slots, heads, width), 0) < live[0]
    for t in range(steps):
        part = rows_ref[pl.ds(t * slots * heads, slots * heads), :].reshape(slots, heads, width)
        out_ref[:, t] = jnp.where(on, part + local_ref[t], 0.0).astype(BF16)


def finish(live, mine, near, far, local):
    steps, slots, heads, width = local.shape
    return pl.pallas_call(
        finish_kernel,
        grid_spec=pltpu.PrefetchScalarGridSpec(
            num_scalar_prefetch=1,
            grid=(1,),
            in_specs=[
                pl.BlockSpec((1,) + mine.shape[1:], lambda i, s: (0, 0, 0, 0)),
                pl.BlockSpec((1,) + near.shape[1:], lambda i, s: (0, 0, 0, 0)),
                pl.BlockSpec((1,) + far.shape[1:], lambda i, s: (0, 0, 0, 0)),
                pl.BlockSpec(local.shape, lambda i, s: (0, 0, 0, 0)),
            ],
            out_specs=pl.BlockSpec((slots, steps, heads, width), lambda i, s: (0, 0, 0, 0)),
            scratch_shapes=[pltpu.VMEM((steps * slots * heads, width), F32)],
        ),
        out_shape=jax.ShapeDtypeStruct((slots, steps, heads, width), BF16),
        compiler_params=pltpu.CompilerParams(vmem_limit_bytes=SMALL_BYTES),
        name="finish",
    )(live, mine, near, far, local)


def shifted(array, by):
    peers = lax.axis_size("dec")
    return lax.ppermute(array, "dec", [(i, i + by) for i in range(peers) if 0 <= i + by < peers])


def added(left, right):
    return (left.astype(F32) + right.astype(F32)).astype(BF16)


def local(
    prompt_query,
    prompt_key,
    prompt_value,
    prompt_beta,
    prompt_gate,
    prompt_lengths,
    request_source_prompt,
    live_counts,
    decode_query,
    decode_key,
    decode_value,
    decode_beta,
    decode_gate,
):
    peers = lax.axis_size("dec")
    tokens = prompt_query.shape[1]
    spans = tokens // SPAN
    steps = decode_query.shape[1]
    longest = peers * spans // 2
    hops = max(1, (longest - 2) // spans + 1)
    probes, decode_local = requests(decode_query, decode_key, decode_value, decode_beta, decode_gate)
    own_probes = [probes]
    for x in range(1, peers):
        pairs = [(i, i ^ reversed_bits(x, peers)) for i in range(peers)]
        own_probes.append(lax.ppermute(probes, "dec", pairs))
    probes, prompt_key = lax.optimization_barrier((probes, prompt_key))
    sources = request_source_prompt.reshape(2, peers, 1, -1)
    slots = sources.shape[3]
    sources = jnp.broadcast_to(sources, (2, peers, steps, slots)).reshape(2, peers, steps * slots, 1)

    chunk_local, chunk_probe, state, first, second, table = prefill(
        prompt_lengths, prompt_query[0], prompt_key[0], prompt_value[0], prompt_beta[0], prompt_gate[0]
    )
    own_probes, first, second = lax.optimization_barrier((own_probes, first, second))
    pairs = [(i, i ^ 1) for i in range(peers)]
    first_got = lax.ppermute(first, "dec", pairs)
    pairs = [(i, (i + 1 ^ 1) - 1) for i in range(1, peers - 1)]
    second_got = lax.ppermute(second, "dec", pairs)
    if hops > 2:
        odd = lax.axis_index("dec") % 2 == 1
        ends = jnp.cumsum(prompt_lengths[0]) - 1
        closed = jnp.any(ends // spans == lax.axis_index("dec"))
        own_map = jnp.where(odd, first, second)
        through = jnp.where(closed, 0.0, own_map.astype(F32)).astype(BF16)

        def turn(_, arriving):
            leaving = state + jnp.einsum("hij,hjk->hik", through, arriving, preferred_element_type=F32)
            return shifted(leaving.astype(BF16), 1)

        arrived = lax.fori_loop(0, hops - 2, turn, jnp.where(odd, first_got, second_got))
        first_got, second_got = (
            jnp.where(odd, arrived, first_got),
            jnp.where(odd, second_got, arrived),
        )
    own_probes = jnp.stack(own_probes)
    other_probes = lax.ppermute(own_probes, "pre", [(0, 1), (1, 0)])
    own_part, other_part = stored_answers(prompt_lengths, spans, table, own_probes, other_probes, sources)
    leaving, keep, send = carried_answers(
        prompt_lengths,
        spans,
        state,
        (first, first_got),
        (second, second_got),
        own_probes,
        other_probes,
        own_part,
        other_part,
        sources,
    )
    theirs = lax.ppermute(send, "pre", [(0, 1), (1, 0)])
    entry = shifted(leaving, 1)
    block = added(keep, theirs)
    theirs = jnp.zeros_like(block)
    bit, part = 1, peers // 2
    while part:
        pairs = [(i, i ^ bit) for i in range(peers)]
        if bit == 1:
            outgoing = block[part:]
        else:
            outgoing = added(block[part : 2 * part], theirs[part : 2 * part])
        if bit > 1 and part > 1:
            block = added(block[:part], theirs[:part])
        before, theirs = theirs, lax.ppermute(outgoing, "dec", pairs)
        bit, part = 2 * bit, part // 2
    step_result = finish(live_counts, block, before, theirs, decode_local)
    prompt_result = emit(chunk_local, chunk_probe, entry)[None]
    return (prompt_result, step_result)


def solution(mesh):
    in_specs = (
        P("pre", "dec", "head", None),
        P("pre", "dec", "head", None),
        P("pre", "dec", "head", None),
        P("pre", "head", "dec"),
        P("pre", "head", "dec"),
        P("pre", None),
        P(),
        P(("pre", "dec")),
        P(("pre", "dec"), None, "head", None),
        P(("pre", "dec"), None, "head", None),
        P(("pre", "dec"), None, "head", None),
        P(("pre", "dec"), None, "head"),
        P(("pre", "dec"), None, "head"),
    )
    out_specs = (P("pre", "dec", "head", None), P(("pre", "dec"), None, "head", None))
    return jax.shard_map(local, mesh=mesh, in_specs=in_specs, out_specs=out_specs, check_vma=False)
```
